32 devices in a mesh: hyp: 2 (over y), row: 4 (over z), col: 4 (over x, core).
Axes of the slice: x: 2, y: 2, z: 4, core: 2. Of those that a mesh axis runs over, the one named last changes fastest.
Arguments:
- inverse_tile: float32 [16384, 8192], P(('hyp', 'row'), 'col'), parts along dimension 0, may hold values from -32768 to 262144, as said below
- panels: float32 [2, 2, 8192, 512], P('hyp', None, ('col', 'row')), parts along dimension 0, may hold values from -0.0007324219 to 0.0007324219
- link_panel: float32 [2, 512, 512], P('hyp'), parts along dimension 0, may hold values from -0.09375 to 0.09375
- diag_inverse: float32 [2, 2, 512, 512], P('hyp', None, 'row', 'col'), parts along dimension 0, may hold values from -3 to 3
- ancestor_tiles: int32 [1, 2, 64], replicated, may hold values 0 or 1
Outputs:
- ancestor_block: float32 [2, 2, 8192, 512], P('hyp', None, ('row', 'col')), parts along dimension 0
- diag_block: float32 [2, 2, 512, 512], P('hyp', None, 'row', 'col'), parts along dimension 0
- cross_block: float32 [2, 512, 512], P('hyp', 'row', 'col'), parts along dimension 0
The draws below stay inside these ranges and needn't reach their ends.
There are 2 independent parts, one for each index of `hyp`. The reference program is written for one: setup_inputs(seed, part) draws one part's arguments, and reference() takes and returns one part's arrays. A program takes and returns all parts, laid end to end along the dimension named above; an argument that names none is the same for every part. Nothing has to cross between parts.
Inputs may be any that keep to these rules, and one draw needn't show every extreme that they name: `inverse_tile`: symmetric.
All inputs are finite; a program needn't handle non-finite values.
Results may differ from the reference program's by a relative error of at most 0.000075.
Values sent between devices are 32-bit elements; how exact they have to be, the bound alone decides.
No kernel may reach another device: no remote copies, remote signals or barrier semaphores. Data moves between devices by JAX's collectives and lax.ppermute only.
A program may use at most 128 MiB of HBM per device.

```python
import jax
import jax.numpy as jnp
from jax import lax

ANC = 8192
B = 512
TILE = 128
SIB = 1
TILES = 64


def draw_inverse_tile(key, part):
    noise_key = jax.random.fold_in(key, 11)
    diag_key = jax.random.fold_in(key, 23)
    noise = jax.random.normal(noise_key, (ANC, ANC), jnp.float32)
    spread = 0.35 * jnp.sqrt(jnp.float32(ANC))
    symmetric = (noise + noise.T) * spread
    diagonal = jax.random.uniform(diag_key, (ANC,), jnp.float32, 1.0, 2.0) * ANC
    matrix = symmetric + jnp.diag(diagonal - jnp.diagonal(symmetric))
    return matrix


def with_ends(values, rng, low, top_value):
    longest = values.shape.index(max(values.shape))
    spots = []
    for shift in (0, 1):
        where = [jax.random.randint(jax.random.fold_in(rng, axis), (), 0, length) for axis, length in enumerate(values.shape)]
        where[longest] = (where[longest] + shift) % values.shape[longest]
        spots.append(tuple(where))
    return values.at[spots[0]].set(low).at[spots[1]].set(top_value)


def shard_levels(stream_key, dims, split, smallest, top_value):
    level = 1.0
    for position, blocks in split:
        steps = jax.random.uniform(jax.random.fold_in(jax.random.fold_in(stream_key, 6), position), (blocks,), jnp.float32, smallest / len(split), top_value / len(split))
        level = level * jnp.repeat(jnp.exp(steps), dims[position] // blocks).reshape((-1,) + (1,) * (len(dims) - 1 - position))
    return level


def normal_values(key, shape, deviation, bound, shards=(), dtype=jnp.bfloat16):
    entries = jax.random.normal(key, shape, jnp.float32) * deviation
    if len(shards) > 0:
        entries = shard_levels(key, shape, shards, -0.22, 0.18) * entries
    return jnp.clip(entries, min=-bound, max=bound).astype(dtype)


def setup_inputs(seed: int = 0, part: int = 0) -> dict:
    seeds = jax.random.split(jax.random.key(seed), 6)
    own_keys = jax.random.split(jax.random.fold_in(seeds[5], part), 6)
    return {
        "inverse_tile": draw_inverse_tile(jax.random.fold_in(jax.random.fold_in(seeds[5], part), 71), part),
        "panels": normal_values(own_keys[1], (SIB, 2, ANC, B), (ANC * ANC) ** -0.5, 0.0007324219, ((2, 16),), jnp.float32),
        "link_panel": normal_values(own_keys[2], (SIB, B, B), (8 * B) ** -0.5, 0.09375, (), jnp.float32),
        "diag_inverse": normal_values(own_keys[3], (SIB, 2, B, B), 0.5, 3.0, ((2, 4), (3, 4)), jnp.float32),
        "ancestor_tiles": with_ends((jax.random.randint(seeds[4], (SIB, 2, TILES), 0, 4) < 3).astype(jnp.int32), jax.random.fold_in(seeds[4], 1), 0, 1),
    }


def reference(inverse_tile, panels, link_panel, diag_inverse, ancestor_tiles):
    precise = lax.Precision.HIGHEST
    rows_kept = jnp.repeat(ancestor_tiles, TILE, axis=2).astype(jnp.float32)
    masked = panels * rows_kept[..., None]
    first = masked[:, 0]
    second = masked[:, 1]
    ancestor_first = -jnp.einsum("ik,skb->sib", inverse_tile, first, precision=precise)
    diag_first = diag_inverse[:, 0] - jnp.einsum("sib,sic->sbc", first, ancestor_first, precision=precise)
    ancestor_second = -(jnp.einsum("ik,skb->sib", inverse_tile, second, precision=precise)
                        + jnp.einsum("sik,skc->sic", ancestor_first, link_panel, precision=precise))
    cross_block = -(jnp.einsum("sib,sic->sbc", ancestor_first, second, precision=precise)
                    + jnp.einsum("sbk,skc->sbc", diag_first, link_panel, precision=precise))
    diag_second = (diag_inverse[:, 1]
                   - jnp.einsum("sib,sic->sbc", second, ancestor_second, precision=precise)
                   - jnp.einsum("skb,skc->sbc", link_panel, cross_block, precision=precise))
    ancestor_block = jnp.stack([ancestor_first, ancestor_second], axis=1)
    diag_block = jnp.stack([diag_first, diag_second], axis=1)
    return ancestor_block, diag_block, cross_block
```

```python
import jax
import jax.numpy as jnp
from jax import lax
from jax.sharding import PartitionSpec as P

TILE = 128

precise = lax.Precision.HIGHEST
three_pass = lax.Precision.HIGH


def swap(block, axis, bit):
    pairs = [(i, i ^ bit) for i in range(lax.axis_size(axis))]
    return lax.ppermute(block, axis, pairs)


def after(block, *others):
    return lax.optimization_barrier((block, *others))[0]


def dot(a, b, precision):
    return jnp.matmul(a, b, precision=precision)


def dot_tn(a, b, precision):
    return lax.dot_general(a, b, (((0,), (0,)), ((), ())), precision=precision)


def split(blocks, axis, bit):
    mine = lax.axis_index(axis) // bit % 2
    pairs = blocks.reshape((blocks.shape[0] // 2, 2) + blocks.shape[1:])
    keep = lax.dynamic_index_in_dim(pairs, mine, 1, keepdims=False)
    send = lax.dynamic_index_in_dim(pairs, 1 - mine, 1, keepdims=False)
    return keep, send


def sum_scatter(blocks, axis, bit=1):
    while bit < lax.axis_size(axis):
        keep, send = split(blocks, axis, bit)
        blocks = keep + swap(send, axis, bit)
        bit *= 2
    return blocks[0]


def gather_blocks(block, axis):
    blocks = {0: block}
    bit = lax.axis_size(axis) // 2
    while bit >= 1:
        blocks.update({j ^ bit: swap(held, axis, bit) for j, held in list(blocks.items())})
        bit //= 2
    return [blocks[j] for j in range(len(blocks))]


def in_order(blocks, axis):
    index = lax.axis_index(axis)
    bit = 1
    while bit < len(blocks):
        flip = index // bit % 2 == 1
        blocks = [jnp.where(flip, blocks[j ^ bit], blocks[j]) for j in range(len(blocks))]
        bit *= 2
    return blocks


def own_output_rows(blocks):
    rows, cols = lax.axis_size("row"), lax.axis_size("col")
    routes = {}
    for r in range(rows):
        for c in range(cols):
            place = r * cols + c
            routes.setdefault((place % rows) ^ r, []).append((r * cols + place // rows, place))
    here = lax.axis_index("row") * cols + lax.axis_index("col")
    total = None
    for j, pairs in sorted(routes.items()):
        moved = [pair for pair in pairs if pair[0] != pair[1]]
        stay = [pair[0] for pair in pairs if pair[0] == pair[1]]
        terms = []
        if moved:
            terms.append(lax.ppermute(blocks[j], ("row", "col"), moved))
        if stay:
            is_here = (here == jnp.array(stay)).any()
            terms.append(jnp.where(is_here, blocks[j], jnp.zeros_like(blocks[j])))
        for term in terms:
            total = term if total is None else total + term
    return total


def local(inverse_tile, panels, link_panel, diag_inverse, ancestor_tiles):
    rows_axis, cols_axis = lax.axis_size("row"), lax.axis_size("col")
    row_id, col_id = lax.axis_index("row"), lax.axis_index("col")
    siblings, _, local_rows, width = panels.shape
    diag_height, diag_span = diag_inverse.shape[2:]
    row_start = (col_id * rows_axis + row_id) * local_rows
    tile_mask = jnp.repeat(ancestor_tiles, TILE, axis=2)
    kept_rows = lax.dynamic_slice_in_dim(tile_mask, row_start, local_rows, 2).astype(jnp.float32)
    masked = panels * kept_rows[..., None]

    out_rows = inverse_tile.shape[0] // cols_axis
    keep_tile, send_tile = split(inverse_tile.reshape(cols_axis, out_rows, -1), "col", 1)
    half_rows = keep_tile.shape[0] * out_rows
    keep_tile = keep_tile.reshape(half_rows, -1)
    send_tile = send_tile.reshape(half_rows, -1)

    chunk = 2 * diag_span
    held = None
    ancestor, diagonals, crosses = [], [], []
    for s in range(siblings):
        link = link_panel[s]
        first = masked[s, 0]
        second = masked[s, 1] - dot(first, link, precise)
        outs, owns = ([], []), ([], [])
        for which, panel in enumerate((first, second)):
            for start in range(0, width, chunk):
                piece = panel[:, start:start + chunk]
                if held is not None:
                    piece = after(piece, held)
                blocks = gather_blocks(piece, "row")
                held = blocks[rows_axis // 2]
                owns[which].append(own_output_rows(blocks))
                column = jnp.concatenate(in_order(blocks, "row"), axis=0)
                sent = swap(dot(send_tile, column, three_pass), "col", 1)
                sums = dot(keep_tile, column, three_pass) + sent
                sums = sum_scatter(sums.reshape(-1, out_rows, chunk), "col", 2)
                outs[which].append(-sums)
        out_first, out_second = (jnp.concatenate(o, axis=1) for o in outs)
        own_first, own_second = (jnp.concatenate(o, axis=1) for o in owns)

        link_cols = lax.dynamic_slice_in_dim(link, col_id * diag_span, diag_span, 1)
        link_rows = lax.dynamic_slice_in_dim(link, row_id * diag_height, diag_height, 0)
        given = jnp.concatenate(in_order(gather_blocks(diag_inverse[s, 0], "col"), "col"), axis=1)
        given_link = dot(given, link_cols, precise)

        def by_cols(terms):
            return terms.reshape(width, cols_axis, diag_span).swapaxes(0, 1)

        def by_rows(terms):
            return terms.reshape(-1, rows_axis, diag_height, diag_span).swapaxes(0, 1)

        early = jnp.stack([by_cols(dot_tn(own_first, out_first, three_pass)),
                           by_cols(dot_tn(out_first, own_second, three_pass))], axis=1)
        early = sum_scatter(by_rows(sum_scatter(early, "col")), "row")
        late = sum_scatter(by_cols(dot_tn(own_second, out_second, three_pass)), "col")
        late = late - dot_tn(link_rows, given_link, precise)
        late = sum_scatter(by_rows(late), "row")

        ancestor.append(jnp.stack([out_first, out_second]))
        diagonals.append(jnp.stack([diag_inverse[s, 0] - early[0], diag_inverse[s, 1] - late[0]]))
        crosses.append(-(early[1] + given_link))
    return jnp.stack(ancestor), jnp.stack(diagonals), jnp.stack(crosses)


def solution(mesh):
    in_specs = (
        P(("hyp", "row"), "col"),
        P("hyp", None, ("col", "row"), None),
        P("hyp", None, None),
        P("hyp", None, "row", "col"),
        P(),
    )
    out_specs = (
        P("hyp", None, ("row", "col"), None),
        P("hyp", None, "row", "col"),
        P("hyp", "row", "col"),
    )
    return jax.shard_map(local, mesh=mesh, in_specs=in_specs, out_specs=out_specs, check_vma=False)
```

```python
import jax
import jax.numpy as jnp
from jax import lax
from jax.sharding import PartitionSpec as P

TILE = 128

precise = lax.Precision.HIGHEST
three_pass = lax.Precision.HIGH


def swap(block, axis, bit):
    pairs = [(i, i ^ bit) for i in range(lax.axis_size(axis))]
    return lax.ppermute(block, axis, pairs)


def after(block, *others):
    return lax.optimization_barrier((block, *others))[0]


def dot(a, b, precision):
    return jnp.matmul(a, b, precision=precision)


def dot_tn(a, b, precision):
    return lax.dot_general(a, b, (((0,), (0,)), ((), ())), precision=precision)


def split(blocks, axis, bit):
    mine = lax.axis_index(axis) // bit % 2
    pairs = blocks.reshape((blocks.shape[0] // 2, 2) + blocks.shape[1:])
    keep = lax.dynamic_index_in_dim(pairs, mine, 1, keepdims=False)
    send = lax.dynamic_index_in_dim(pairs, 1 - mine, 1, keepdims=False)
    return keep, send


def sum_scatter(blocks, axis, bit=1):
    while bit < lax.axis_size(axis):
        keep, send = split(blocks, axis, bit)
        blocks = keep + swap(send, axis, bit)
        bit *= 2
    return blocks[0]


def gather_blocks(block, axis):
    blocks = {0: block}
    bit = lax.axis_size(axis) // 2
    while bit >= 1:
        blocks.update({j ^ bit: swap(held, axis, bit) for j, held in list(blocks.items())})
        bit //= 2
    return [blocks[j] for j in range(len(blocks))]


def placed(blocks, axis):
    index = lax.axis_index(axis)
    height = blocks[0].shape[0]
    whole = jnp.zeros((len(blocks) * height,) + blocks[0].shape[1:], blocks[0].dtype)
    for j, block in enumerate(blocks):
        whole = lax.dynamic_update_slice_in_dim(whole, block, (index ^ j) * height, 0)
    return whole


def all_sum(block, axis):
    bit = 1
    while bit < lax.axis_size(axis):
        block = block + swap(block, axis, bit)
        bit *= 2
    return block


def source_col(row):
    return row * lax.axis_size("col") // lax.axis_size("row")


def own_output_rows(blocks):
    rows, cols = lax.axis_size("row"), lax.axis_size("col")
    row_id, col_id = lax.axis_index("row"), lax.axis_index("col")
    offset = col_id ^ source_col(row_id)
    held = []
    for d in range(cols):
        wanted = [((r * cols + (source_col(r) ^ d)) % rows) ^ r for r in range(rows)]
        if len(set(wanted)) == 1:
            held.append(blocks[wanted[0]])
        else:
            held.append(lax.dynamic_index_in_dim(jnp.stack(blocks), jnp.array(wanted)[row_id], 0, keepdims=False))
    bit = cols // 2
    while bit >= 1:
        pairs = [(r * cols + c, r * cols + (c ^ bit)) for r in range(rows) for c in range(cols)
                 if (c ^ source_col(r)) % (2 * bit) == 0]
        moved = lax.ppermute(jnp.stack(held[bit:]), ("row", "col"), pairs)
        held = [jnp.where(offset & bit != 0, moved[j], held[j]) for j in range(bit)]
        bit //= 2
    return held[0]


def own_output_rows_direct(block):
    rows, cols = lax.axis_size("row"), lax.axis_size("col")
    pairs = [(r * cols + c, c * rows + r) for r in range(rows) for c in range(cols)]
    return lax.ppermute(block, ("row", "col"), pairs)


def local(inverse_tile, panels, link_panel, diag_inverse, ancestor_tiles):
    rows_axis, cols_axis = lax.axis_size("row"), lax.axis_size("col")
    row_id, col_id = lax.axis_index("row"), lax.axis_index("col")
    siblings, _, local_rows, width = panels.shape
    height, span = diag_inverse.shape[2:]
    row_start = (col_id * rows_axis + row_id) * local_rows
    tile_mask = jnp.repeat(ancestor_tiles, TILE, axis=2)
    kept_rows = lax.dynamic_slice_in_dim(tile_mask, row_start, local_rows, 2).astype(jnp.float32)
    masked = panels * kept_rows[..., None]

    out_rows = inverse_tile.shape[0] // cols_axis
    keep_tile, send_tile = split(inverse_tile.reshape(cols_axis, out_rows, -1), "col", 1)
    half_rows = keep_tile.shape[0] * out_rows
    keep_tile = keep_tile.reshape(half_rows, -1)
    send_tile = send_tile.reshape(half_rows, -1)

    def product(blocks):
        column = placed(blocks, "row")
        sent = swap(dot(send_tile, column, three_pass), "col", 1)
        sums = dot(keep_tile, column, three_pass) + sent
        return -sum_scatter(sums.reshape(-1, out_rows, column.shape[1]), "col", 2)

    def by_cols(terms):
        return terms.reshape(width, cols_axis, -1).swapaxes(0, 1)

    def by_rows(terms):
        return terms.reshape(rows_axis, height, -1)

    def spread_sum(terms):
        terms = jnp.concatenate([by_cols(term) for term in terms], axis=2)
        terms = lax.psum_scatter(terms, "col", scatter_dimension=0)
        terms = lax.psum_scatter(by_rows(terms), "row", scatter_dimension=0)
        return [terms[:, start:start + span] for start in range(0, terms.shape[1], span)]

    late = 2 * span
    sent = []
    ancestor, diagonals, crosses = [], [], []
    for s in range(siblings):
        link = link_panel[s]
        first = masked[s, 0]
        second = masked[s, 1] - dot(first, link, precise)

        def gathered(panel, start, stop):
            piece = panel[:, start:stop]
            if len(sent) >= 2:
                piece = after(piece, sent[-2])
            blocks = gather_blocks(piece, "row")
            sent.append(blocks[rows_axis // 2])
            return blocks

        def joined(groups):
            return [jnp.concatenate(group, axis=1) for group in zip(*groups)]

        first_blocks = [gathered(first, i, i + late) for i in range(0, width, late)]
        second_blocks = [gathered(second, i, i + late) for i in range(0, width - late, late)]
        last_blocks = [gathered(second, i, i + span) for i in range(width - late, width, span)]
        own_last = own_output_rows_direct(after(second[:, width - late:], sent[1]))

        link_cols = lax.dynamic_slice_in_dim(link, col_id * span, span, 1)
        link_rows = lax.dynamic_slice_in_dim(link, row_id * height, height, 0)
        given = placed([block.T for block in gather_blocks(diag_inverse[s, 0], "col")], "col")
        given_link = dot_tn(given, link_cols, precise)

        out_first = jnp.concatenate([product(blocks) for blocks in first_blocks], axis=1)
        own_first = own_output_rows(joined(first_blocks))
        (first_sum,) = spread_sum([dot_tn(own_first, out_first, three_pass)])

        out_early = jnp.concatenate([product(blocks) for blocks in second_blocks], axis=1)
        own_early = own_output_rows(joined(second_blocks))
        own_second = jnp.concatenate([own_early, own_last], axis=1)
        cross_terms = dot_tn(out_first, own_second, three_pass)
        early_terms = jnp.concatenate([
            dot_tn(own_second, out_early, three_pass),
            jnp.pad(dot_tn(out_early, own_last, three_pass), ((0, late), (0, 0)))], axis=1)
        cross_sum, early_sum = spread_sum([cross_terms, early_terms])

        link_terms = lax.psum_scatter(by_rows(dot_tn(link_rows, given_link, precise)), "row", scatter_dimension=0)

        out_a = product(last_blocks[0])
        terms_a = all_sum(all_sum(dot_tn(own_last, out_a, three_pass), "col"), "row")
        out_b = product(last_blocks[1])
        terms_b = all_sum(all_sum(dot_tn(own_last[:, span:], out_b, three_pass), "col"), "row")
        last_terms = jnp.concatenate([
            terms_a, jnp.concatenate([terms_a[span:].T, terms_b], axis=0)], axis=1)
        padded = jnp.pad(last_terms, ((height, 0), (span, 0)))
        corner = width - late
        last_sum = lax.dynamic_slice(
            padded,
            (jnp.maximum(row_id * height - corner + height, 0), jnp.maximum(col_id * span - corner + span, 0)),
            (height, span))

        ancestor.append(jnp.stack([out_first, jnp.concatenate([out_early, out_a, out_b], axis=1)]))
        diagonals.append(jnp.stack([
            diag_inverse[s, 0] - first_sum,
            diag_inverse[s, 1] - early_sum - last_sum + link_terms]))
        crosses.append(-(cross_sum + given_link))
    return jnp.stack(ancestor), jnp.stack(diagonals), jnp.stack(crosses)


def solution(mesh):
    in_specs = (
        P(("hyp", "row"), "col"),
        P("hyp", None, ("col", "row"), None),
        P("hyp", None, None),
        P("hyp", None, "row", "col"),
        P(),
    )
    out_specs = (
        P("hyp", None, ("row", "col"), None),
        P("hyp", None, "row", "col"),
        P("hyp", "row", "col"),
    )
    return jax.shard_map(local, mesh=mesh, in_specs=in_specs, out_specs=out_specs, check_vma=False)
```

```python
import jax
import jax.numpy as jnp
from jax import lax
from jax.experimental import pallas as pl
from jax.experimental.pallas import tpu as pltpu
from jax.sharding import PartitionSpec as P

TILE = 128

precise = lax.Precision.HIGHEST
three_pass = lax.Precision.HIGH


def swap(block, axis, bit):
    pairs = [(i, i ^ bit) for i in range(lax.axis_size(axis))]
    return lax.ppermute(block, axis, pairs)


def parts(values):
    high = values.astype(jnp.bfloat16)
    return high, (values - high.astype(jnp.float32)).astype(jnp.bfloat16)


def product_kernel(place, tile_ref, *refs):
    *block_refs, out_ref, high_ref, low_ref = refs
    height = block_refs[0].shape[0]

    @pl.when((pl.program_id(0) == 0) & (pl.program_id(1) == 0))
    def _():
        for j, block_ref in enumerate(block_refs):
            rows = pl.ds(pl.multiple_of((place[0] ^ j) * height, height), height)
            high_ref[rows], low_ref[rows] = parts(block_ref[...])

    high, low = parts(tile_ref[0])
    out_ref[0] = (jnp.dot(high, high_ref[...], preferred_element_type=jnp.float32)
                  + (jnp.dot(high, low_ref[...], preferred_element_type=jnp.float32)
                     + jnp.dot(low, high_ref[...], preferred_element_type=jnp.float32)))


def product(tile, blocks, parity):
    count, out_rows, width = tile.shape
    columns = blocks[0].shape[1]
    step = min(out_rows, 256)
    chunks = lax.axis_index("col") ^ (2 * jnp.arange(count // 2) + parity)
    place = jnp.concatenate([lax.axis_index("row")[None], chunks]).astype(jnp.int32)
    whole = pl.BlockSpec(blocks[0].shape, lambda i, t, place: (0, 0))
    return pl.pallas_call(
        product_kernel,
        grid_spec=pltpu.PrefetchScalarGridSpec(
            num_scalar_prefetch=1,
            grid=(count // 2, out_rows // step),
            in_specs=[pl.BlockSpec((1, step, width), lambda i, t, place: (place[1 + i], t, 0))]
            + [whole] * len(blocks),
            out_specs=pl.BlockSpec((1, step, columns), lambda i, t, place: (i, t, 0)),
            scratch_shapes=[pltpu.VMEM((width, columns), jnp.bfloat16)] * 2,
        ),
        out_shape=jax.ShapeDtypeStruct((count // 2, out_rows, columns), jnp.float32),
        compiler_params=pltpu.CompilerParams(vmem_limit_bytes=40 * 2**20),
    )(place, tile, *blocks)


def after(block, *others):
    return lax.optimization_barrier((block, *others))[0]


def dot(a, b, precision):
    return jnp.matmul(a, b, precision=precision)


def dot_tn(a, b, precision):
    return lax.dot_general(a, b, (((0,), (0,)), ((), ())), precision=precision)


def sum_scatter(blocks, axis, bit=1):
    while blocks.shape[0] > 1:
        pairs = blocks.reshape((blocks.shape[0] // 2, 2) + blocks.shape[1:])
        blocks = pairs[:, 0] + swap(pairs[:, 1], axis, bit)
        bit *= 2
    return blocks[0]


def by_xor(blocks, axis):
    index = lax.axis_index(axis)
    return jnp.stack([lax.dynamic_index_in_dim(blocks, index ^ j, 0, keepdims=False)
                      for j in range(blocks.shape[0])])


def gather_blocks(block, axis):
    blocks = {0: block}
    bit = lax.axis_size(axis) // 2
    while bit >= 1:
        blocks.update({j ^ bit: swap(held, axis, bit) for j, held in list(blocks.items())})
        bit //= 2
    return [blocks[j] for j in range(len(blocks))]


def placed(blocks, axis):
    index = lax.axis_index(axis)
    height = blocks[0].shape[0]
    whole = jnp.zeros((len(blocks) * height,) + blocks[0].shape[1:], blocks[0].dtype)
    for j, block in enumerate(blocks):
        whole = lax.dynamic_update_slice_in_dim(whole, block, (index ^ j) * height, 0)
    return whole


def all_sum(block, axis):
    bit = 1
    while bit < lax.axis_size(axis):
        block = block + swap(block, axis, bit)
        bit *= 2
    return block


def source_col(row):
    return row * lax.axis_size("col") // lax.axis_size("row")


def own_output_rows(blocks):
    rows, cols = lax.axis_size("row"), lax.axis_size("col")
    row_id, col_id = lax.axis_index("row"), lax.axis_index("col")
    offset = col_id ^ source_col(row_id)
    held = []
    for d in range(cols):
        wanted = [((r * cols + (source_col(r) ^ d)) % rows) ^ r for r in range(rows)]
        if len(set(wanted)) == 1:
            held.append(blocks[wanted[0]])
        else:
            held.append(lax.dynamic_index_in_dim(jnp.stack(blocks), jnp.array(wanted)[row_id], 0, keepdims=False))
    bit = cols // 2
    while bit >= 1:
        pairs = [(r * cols + c, r * cols + (c ^ bit)) for r in range(rows) for c in range(cols)
                 if (c ^ source_col(r)) % (2 * bit) == 0]
        moved = lax.ppermute(jnp.stack(held[bit:]), ("row", "col"), pairs)
        held = [jnp.where(offset & bit != 0, moved[j], held[j]) for j in range(bit)]
        bit //= 2
    return held[0]


def own_output_rows_direct(block):
    rows, cols = lax.axis_size("row"), lax.axis_size("col")
    pairs = [(r * cols + c, c * rows + r) for r in range(rows) for c in range(cols)]
    return lax.ppermute(block, ("row", "col"), pairs)


def local(inverse_tile, panels, link_panel, diag_inverse, ancestor_tiles):
    rows_axis, cols_axis = lax.axis_size("row"), lax.axis_size("col")
    row_id, col_id = lax.axis_index("row"), lax.axis_index("col")
    siblings, _, local_rows, width = panels.shape
    height, span = diag_inverse.shape[2:]
    row_start = (col_id * rows_axis + row_id) * local_rows
    tile_mask = jnp.repeat(ancestor_tiles, TILE, axis=2)
    kept_rows = lax.dynamic_slice_in_dim(tile_mask, row_start, local_rows, 2).astype(jnp.float32)
    masked = panels * kept_rows[..., None]

    tile = inverse_tile.reshape(cols_axis, inverse_tile.shape[0] // cols_axis, -1)

    def output_rows(blocks):
        sent = swap(product(tile, blocks, 1), "col", 1)
        return -sum_scatter(product(tile, blocks, 0) + sent, "col", 2)

    def by_cols(terms):
        return terms.reshape(width, cols_axis, -1).swapaxes(0, 1)

    def by_rows(terms):
        return terms.reshape(rows_axis, height, -1)

    def spread_sum(terms):
        terms = jnp.concatenate([by_cols(term) for term in terms], axis=2)
        terms = sum_scatter(by_xor(terms, "col"), "col")
        terms = sum_scatter(by_xor(by_rows(terms), "row"), "row")
        return [terms[:, start:start + span] for start in range(0, terms.shape[1], span)]

    late = 2 * span
    sent = []
    ancestor, diagonals, crosses = [], [], []
    for s in range(siblings):
        link = link_panel[s]
        first = masked[s, 0]
        second = masked[s, 1] - dot(first, link, precise)

        def gathered(panel, start, stop):
            piece = panel[:, start:stop]
            if len(sent) >= 2:
                piece = after(piece, sent[-2])
            blocks = gather_blocks(piece, "row")
            sent.append(blocks[rows_axis // 2])
            return blocks

        def joined(groups):
            return [jnp.concatenate(group, axis=1) for group in zip(*groups)]

        first_blocks = [gathered(first, i, i + late) for i in range(0, width, late)]
        second_blocks = [gathered(second, i, i + late) for i in range(0, width - late, late)]
        last_blocks = [gathered(second, i, i + span) for i in range(width - late, width, span)]
        own_last = own_output_rows_direct(after(second[:, width - late:], sent[1]))

        link_cols = lax.dynamic_slice_in_dim(link, col_id * span, span, 1)
        link_rows = lax.dynamic_slice_in_dim(link, row_id * height, height, 0)
        given = placed([block.T for block in gather_blocks(diag_inverse[s, 0], "col")], "col")
        given_link = dot_tn(given, link_cols, precise)

        out_first = jnp.concatenate([output_rows(blocks) for blocks in first_blocks], axis=1)
        own_first = own_output_rows(joined(first_blocks))
        (first_sum,) = spread_sum([dot_tn(own_first, out_first, three_pass)])

        out_early = jnp.concatenate([output_rows(blocks) for blocks in second_blocks], axis=1)
        own_early = own_output_rows(joined(second_blocks))
        own_second = jnp.concatenate([own_early, own_last], axis=1)
        cross_terms = dot_tn(out_first, own_second, three_pass)
        early_terms = jnp.concatenate([
            dot_tn(own_second, out_early, three_pass),
            jnp.pad(dot_tn(out_early, own_last, three_pass), ((0, late), (0, 0)))], axis=1)
        cross_sum, early_sum = spread_sum([cross_terms, early_terms])

        link_terms = sum_scatter(by_xor(by_rows(dot_tn(link_rows, given_link, precise)), "row"), "row")

        out_a = output_rows(last_blocks[0])
        terms_a = all_sum(all_sum(dot_tn(own_last, out_a, three_pass), "col"), "row")
        out_b = output_rows(last_blocks[1])
        terms_b = all_sum(all_sum(dot_tn(own_last[:, span:], out_b, three_pass), "col"), "row")
        last_terms = jnp.concatenate([
            terms_a, jnp.concatenate([terms_a[span:].T, terms_b], axis=0)], axis=1)
        padded = jnp.pad(last_terms, ((height, 0), (span, 0)))
        corner = width - late
        last_sum = lax.dynamic_slice(
            padded,
            (jnp.maximum(row_id * height - corner + height, 0), jnp.maximum(col_id * span - corner + span, 0)),
            (height, span))

        ancestor.append(jnp.stack([out_first, jnp.concatenate([out_early, out_a, out_b], axis=1)]))
        diagonals.append(jnp.stack([
            diag_inverse[s, 0] - first_sum,
            diag_inverse[s, 1] - early_sum - last_sum + link_terms]))
        crosses.append(-(cross_sum + given_link))
    return jnp.stack(ancestor), jnp.stack(diagonals), jnp.stack(crosses)


def solution(mesh):
    in_specs = (
        P(("hyp", "row"), "col"),
        P("hyp", None, ("col", "row"), None),
        P("hyp", None, None),
        P("hyp", None, "row", "col"),
        P(),
    )
    out_specs = (
        P("hyp", None, ("row", "col"), None),
        P("hyp", None, "row", "col"),
        P("hyp", "row", "col"),
    )
    return jax.shard_map(local, mesh=mesh, in_specs=in_specs, out_specs=out_specs, check_vma=False)
```

```python
import jax
import jax.numpy as jnp
from jax import lax
from jax.experimental import pallas as pl
from jax.experimental.pallas import tpu as pltpu
from jax.sharding import PartitionSpec as P

TILE = 128

precise = lax.Precision.HIGHEST
three_pass = lax.Precision.HIGH


def swap(block, axis, bit):
    pairs = [(i, i ^ bit) for i in range(lax.axis_size(axis))]
    return lax.ppermute(block, axis, pairs)


def parts(values):
    high = values.astype(jnp.bfloat16)
    return high, (values - high.astype(jnp.float32)).astype(jnp.bfloat16)


def product_kernel(place, tile_ref, *refs):
    *block_refs, out_ref, high_ref, low_ref = refs
    height = block_refs[0].shape[0]

    @pl.when((pl.program_id(0) == 0) & (pl.program_id(1) == 0))
    def _():
        for j, block_ref in enumerate(block_refs):
            rows = pl.ds(pl.multiple_of((place[0] ^ j) * height, height), height)
            high_ref[rows], low_ref[rows] = parts(block_ref[...])

    high, low = parts(tile_ref[0])
    out_ref[0] = (jnp.dot(high, high_ref[...], preferred_element_type=jnp.float32)
                  + (jnp.dot(high, low_ref[...], preferred_element_type=jnp.float32)
                     + jnp.dot(low, high_ref[...], preferred_element_type=jnp.float32)))


def product(tile, blocks, parity):
    count, out_rows, width = tile.shape
    columns = blocks[0].shape[1]
    step = min(out_rows, 256)
    chunks = lax.axis_index("col") ^ (2 * jnp.arange(count // 2) + parity)
    place = jnp.concatenate([lax.axis_index("row")[None], chunks]).astype(jnp.int32)
    whole = pl.BlockSpec(blocks[0].shape, lambda i, t, place: (0, 0))
    return pl.pallas_call(
        product_kernel,
        grid_spec=pltpu.PrefetchScalarGridSpec(
            num_scalar_prefetch=1,
            grid=(count // 2, out_rows // step),
            in_specs=[pl.BlockSpec((1, step, width), lambda i, t, place: (place[1 + i], t, 0))]
            + [whole] * len(blocks),
            out_specs=pl.BlockSpec((1, step, columns), lambda i, t, place: (i, t, 0)),
            scratch_shapes=[pltpu.VMEM((width, columns), jnp.bfloat16)] * 2,
        ),
        out_shape=jax.ShapeDtypeStruct((count // 2, out_rows, columns), jnp.float32),
        compiler_params=pltpu.CompilerParams(vmem_limit_bytes=40 * 2**20),
    )(place, tile, *blocks)


def dot(a, b, precision):
    return jnp.matmul(a, b, precision=precision)


def dot_tn(a, b, precision):
    return lax.dot_general(a, b, (((0,), (0,)), ((), ())), precision=precision)


def sum_scatter(blocks, axis, bit=1):
    while blocks.shape[0] > 1:
        pairs = blocks.reshape((blocks.shape[0] // 2, 2) + blocks.shape[1:])
        blocks = pairs[:, 0] + swap(pairs[:, 1], axis, bit)
        bit *= 2
    return blocks[0]


def by_xor(blocks, axis):
    index = lax.axis_index(axis)
    return jnp.stack([lax.dynamic_index_in_dim(blocks, index ^ j, 0, keepdims=False)
                      for j in range(blocks.shape[0])])


def placed(blocks, axis):
    index = lax.axis_index(axis)
    height = blocks[0].shape[0]
    whole = jnp.zeros((len(blocks) * height,) + blocks[0].shape[1:], blocks[0].dtype)
    for j, block in enumerate(blocks):
        whole = lax.dynamic_update_slice_in_dim(whole, block, (index ^ j) * height, 0)
    return whole


def sum_to_last(block, axis, count):
    size = lax.axis_size(axis)
    bit = 1
    while bit < size:
        if bit * count >= size:
            block = block + lax.ppermute(block, axis, [(i, i ^ bit) for i in range(size) if not i & bit])
        else:
            block = block + swap(block, axis, bit)
        bit *= 2
    return block


def source_col(row):
    return row * lax.axis_size("col") // lax.axis_size("row")


def own_output_rows(blocks):
    rows, cols = lax.axis_size("row"), lax.axis_size("col")
    row_id, col_id = lax.axis_index("row"), lax.axis_index("col")
    offset = col_id ^ source_col(row_id)
    held = []
    for d in range(cols):
        wanted = [((r * cols + (source_col(r) ^ d)) % rows) ^ r for r in range(rows)]
        if len(set(wanted)) == 1:
            held.append(blocks[wanted[0]])
        else:
            held.append(lax.dynamic_index_in_dim(jnp.stack(blocks), jnp.array(wanted)[row_id], 0, keepdims=False))
    bit = cols // 2
    while bit >= 1:
        pairs = [(r * cols + c, r * cols + (c ^ bit)) for r in range(rows) for c in range(cols)
                 if (c ^ source_col(r)) % (2 * bit) == 0]
        moved = lax.ppermute(jnp.stack(held[bit:]), ("row", "col"), pairs)
        held = [jnp.where(offset & bit != 0, moved[j], held[j]) for j in range(bit)]
        bit //= 2
    return held[0]


def own_output_rows_direct(block):
    rows, cols = lax.axis_size("row"), lax.axis_size("col")
    pairs = [(r * cols + c, c * rows + r) for r in range(rows) for c in range(cols)]
    return lax.ppermute(block, ("row", "col"), pairs)


def local(inverse_tile, panels, link_panel, diag_inverse, ancestor_tiles):
    rows_axis, cols_axis = lax.axis_size("row"), lax.axis_size("col")
    row_id, col_id = lax.axis_index("row"), lax.axis_index("col")
    siblings, _, local_rows, width = panels.shape
    height, span = diag_inverse.shape[2:]
    row_start = (col_id * rows_axis + row_id) * local_rows
    tile_mask = jnp.repeat(ancestor_tiles, TILE, axis=2)
    kept_rows = lax.dynamic_slice_in_dim(tile_mask, row_start, local_rows, 2).astype(jnp.float32)
    masked = panels * kept_rows[..., None]
    tile = inverse_tile.reshape(cols_axis, inverse_tile.shape[0] // cols_axis, -1)

    def by_cols(*terms):
        terms = jnp.concatenate([term.reshape(width, cols_axis, span).swapaxes(0, 1) for term in terms], axis=2)
        return by_xor(terms, "col")

    def by_rows(terms):
        return by_xor(terms.reshape(rows_axis, height, -1), "row")

    def one_pair(first, panel_second, link, given_first, given_second):
        live = {"first": first, "second": panel_second - dot(first, link, precise)}
        slots = {}

        def at(slot, *steps):
            slots.setdefault(slot, []).extend(steps)

        late = 2 * span
        pieces = [("first", i, i + late) for i in range(0, width, late)]
        count_first = len(pieces)
        pieces += [("second", i, i + late) for i in range(0, width - late, late)]
        count_early = len(pieces)
        pieces += [("second", i, i + span) for i in range(width - late, width, span)]
        stages = rows_axis.bit_length() - 1

        def fetch(k, stage):
            if stage == 0:
                panel, start, stop = pieces[k]
                live[k, 0] = live[panel][:, start:stop]
            for j in range(1, rows_axis):
                if j.bit_count() == stage + 1:
                    live[k, j] = swap(live[k, j & (j - 1)], "row", j & -j)

        def blocks(k):
            return [live[k, j] for j in range(rows_axis)]

        def multiply(k):
            sent = swap(product(tile, blocks(k), 1), "col", 1)
            live["sums", k] = product(tile, blocks(k), 0) + sent

        def reduce(k):
            live["out", k] = -sum_scatter(live.pop(("sums", k)), "col", 2)

        def own(name, start, stop):
            groups = zip(*(blocks(k) for k in range(start, stop)))
            live[name] = own_output_rows([jnp.concatenate(group, axis=1) for group in groups])
            for k in range(start, stop):
                for j in range(rows_axis):
                    del live[k, j]

        def outs(start, stop):
            return jnp.concatenate([live["out", k] for k in range(start, stop)], axis=1)

        for k in range(len(pieces)):
            for stage in range(stages):
                at(k + stage, lambda k=k, stage=stage: fetch(k, stage))

        def own_last():
            live["own_last"] = own_output_rows_direct(live["second"][:, width - late:])

        def given_link():
            link_cols = lax.dynamic_slice_in_dim(link, col_id * span, span, 1)
            given = {0: given_first}
            bit = cols_axis // 2
            while bit >= 1:
                given.update({j ^ bit: swap(block, "col", bit) for j, block in list(given.items())})
                bit //= 2
            given = [given[j].T for j in range(cols_axis)]
            live["given_link"] = dot_tn(placed(given, "col"), link_cols, precise)

        def first_terms():
            live["first_terms"] = sum_scatter(
                by_cols(dot_tn(live["own_first"], outs(0, count_first), three_pass)), "col")

        def first_sum():
            live["first_sum"] = sum_scatter(by_rows(live.pop("first_terms")), "row")

        def early_terms():
            out_early = outs(count_first, count_early)
            own_second = jnp.concatenate([live["own_early"], live["own_last"]], axis=1)
            cross = dot_tn(outs(0, count_first), own_second, three_pass)
            early = jnp.concatenate([
                dot_tn(own_second, out_early, three_pass),
                jnp.pad(dot_tn(out_early, live["own_last"], three_pass), ((0, late), (0, 0)))], axis=1)
            live["early_terms"] = sum_scatter(by_cols(cross, early), "col")

        def early_sum():
            link_rows = lax.dynamic_slice_in_dim(link, row_id * height, height, 0)
            terms = live.pop("early_terms")
            terms = terms.at[:, span:].add(-dot_tn(link_rows, live["given_link"], precise))
            live["early_sum"] = sum_scatter(by_rows(terms), "row")

        def last_terms(k):
            start = (k - count_early) * span
            terms = dot_tn(live["own_last"][:, start:], live["out", k], three_pass)
            count = cols_axis * terms.shape[1] // terms.shape[0]
            live["last", k] = sum_to_last(sum_to_last(terms, "col", count), "row", count)

        end = len(pieces) - 1 + stages
        for k in range(len(pieces)):
            at(k + stages, lambda k=k: multiply(k))
            at(min(k + stages + 1, end), lambda k=k: reduce(k))
            if k == 0:
                at(1, own_last)
                at(1, given_link)
            if k == count_first - 1:
                at(k + stages, lambda: own("own_first", 0, count_first))
                at(k + stages + 1, first_terms)
                at(k + stages + 2, first_sum)
            if k == count_early - 1:
                at(k + stages, lambda: own("own_early", count_first, count_early))
                at(k + stages + 1, early_terms)
                at(k + stages + 2, early_sum)
            if k >= count_early:
                at(end, lambda k=k: last_terms(k))

        for slot in range(end + 1):
            if slot > 0:
                live = dict(zip(live, lax.optimization_barrier(tuple(live.values()))))
            for step in slots[slot]:
                step()

        last_a, last_b = live["last", end - stages - 1], live["last", end - stages]
        last = jnp.concatenate([last_a, jnp.concatenate([last_a[span:].T, last_b], axis=0)], axis=1)
        padded = jnp.pad(last, ((height, 0), (span, 0)))
        corner = width - late
        last_sum = lax.dynamic_slice(
            padded,
            (jnp.maximum(row_id * height - corner + height, 0), jnp.maximum(col_id * span - corner + span, 0)),
            (height, span))
        cross_sum, early = live["early_sum"][:, :span], live["early_sum"][:, span:]
        ancestor = jnp.stack([outs(0, count_first), outs(count_first, len(pieces))])
        diagonal = jnp.stack([given_first - live["first_sum"], given_second - early - last_sum])
        return ancestor, diagonal, -(cross_sum + live["given_link"])

    results = [one_pair(masked[s, 0], masked[s, 1], link_panel[s], diag_inverse[s, 0], diag_inverse[s, 1])
               for s in range(siblings)]
    return tuple(jnp.stack(group) for group in zip(*results))


def solution(mesh):
    in_specs = (
        P(("hyp", "row"), "col"),
        P("hyp", None, ("col", "row"), None),
        P("hyp", None, None),
        P("hyp", None, "row", "col"),
        P(),
    )
    out_specs = (
        P("hyp", None, ("row", "col"), None),
        P("hyp", None, "row", "col"),
        P("hyp", "row", "col"),
    )
    return jax.shard_map(local, mesh=mesh, in_specs=in_specs, out_specs=out_specs, check_vma=False)
```

```python
import jax
import jax.numpy as jnp
from jax import lax
from jax.experimental import pallas as pl
from jax.experimental.pallas import tpu as pltpu
from jax.sharding import PartitionSpec as P

TILE = 128

precise = lax.Precision.HIGHEST
three_pass = lax.Precision.HIGH


def swap(block, axis, bit):
    pairs = [(i, i ^ bit) for i in range(lax.axis_size(axis))]
    return lax.ppermute(block, axis, pairs)


def parts(values):
    high = values.astype(jnp.bfloat16)
    return high, (values - high.astype(jnp.float32)).astype(jnp.bfloat16)


def split_kernel(tile_ref, high_ref, low_ref):
    high_ref[...], low_ref[...] = parts(tile_ref[...])


def split(tile):
    rows, width = tile.shape
    step = min(rows, 256)
    block = pl.BlockSpec((step, width), lambda t: (t, 0))
    return pl.pallas_call(
        split_kernel,
        grid=(rows // step,),
        in_specs=[block],
        out_specs=[block, block],
        out_shape=[jax.ShapeDtypeStruct(tile.shape, jnp.bfloat16)] * 2,
        compiler_params=pltpu.CompilerParams(vmem_limit_bytes=40 * 2**20),
    )(tile)


def product_kernel(place, tile_high_ref, tile_low_ref, *refs):
    *block_refs, send_ref, keep_ref, high_ref, low_ref = refs
    height = block_refs[0].shape[0]
    i = pl.program_id(0)

    @pl.when(i == 0)
    def _():
        for j, block_ref in enumerate(block_refs):
            rows = pl.ds(pl.multiple_of((place[0] ^ j) * height, height), height)
            high_ref[rows], low_ref[rows] = parts(block_ref[...])

    def times(a_ref, b_ref):
        return jnp.dot(a_ref[0], b_ref[...], preferred_element_type=jnp.float32)

    result = times(tile_high_ref, high_ref) + (times(tile_high_ref, low_ref) + times(tile_low_ref, high_ref))

    @pl.when(i < pl.num_programs(0) // 2)
    def _():
        send_ref[0] = result

    @pl.when(i >= pl.num_programs(0) // 2)
    def _():
        keep_ref[0] = result


def product(tiles, blocks):
    count, out_rows, width = tiles[0].shape
    columns = blocks[0].shape[1]
    half = count // 2
    chunks = lax.axis_index("col") ^ jnp.concatenate([2 * jnp.arange(half) + 1, 2 * jnp.arange(half)])
    place = jnp.concatenate([lax.axis_index("row")[None], chunks]).astype(jnp.int32)
    whole = pl.BlockSpec(blocks[0].shape, lambda i, place: (0, 0))
    rows = pl.BlockSpec((1, out_rows, width), lambda i, place: (place[1 + i], 0, 0))
    return pl.pallas_call(
        product_kernel,
        grid_spec=pltpu.PrefetchScalarGridSpec(
            num_scalar_prefetch=1,
            grid=(count,),
            in_specs=[rows, rows] + [whole] * len(blocks),
            out_specs=[pl.BlockSpec((1, out_rows, columns), lambda i, place: (jnp.minimum(i, half - 1), 0, 0)),
                       pl.BlockSpec((1, out_rows, columns), lambda i, place: (jnp.maximum(i - half, 0), 0, 0))],
            scratch_shapes=[pltpu.VMEM((width, columns), jnp.bfloat16)] * 2,
        ),
        out_shape=[jax.ShapeDtypeStruct((half, out_rows, columns), jnp.float32)] * 2,
        compiler_params=pltpu.CompilerParams(vmem_limit_bytes=40 * 2**20),
    )(place, *tiles, *blocks)


def dot(a, b, precision):
    return jnp.matmul(a, b, precision=precision)


def dot_tn(a, b, precision):
    return lax.dot_general(a, b, (((0,), (0,)), ((), ())), precision=precision)


def sum_scatter(blocks, axis, bit=1):
    while blocks.shape[0] > 1:
        pairs = blocks.reshape((blocks.shape[0] // 2, 2) + blocks.shape[1:])
        blocks = pairs[:, 0] + swap(pairs[:, 1], axis, bit)
        bit *= 2
    return blocks[0]


def by_xor(blocks, axis):
    index = lax.axis_index(axis)
    return jnp.stack([lax.dynamic_index_in_dim(blocks, index ^ j, 0, keepdims=False)
                      for j in range(blocks.shape[0])])


def placed(blocks, axis):
    index = lax.axis_index(axis)
    height = blocks[0].shape[0]
    whole = jnp.zeros((len(blocks) * height,) + blocks[0].shape[1:], blocks[0].dtype)
    for j, block in enumerate(blocks):
        whole = lax.dynamic_update_slice_in_dim(whole, block, (index ^ j) * height, 0)
    return whole


def sum_to_last(block, axis, count):
    size = lax.axis_size(axis)
    bit = 1
    while bit < size:
        if bit * count >= size:
            block = block + lax.ppermute(block, axis, [(i, i ^ bit) for i in range(size) if not i & bit])
        else:
            block = block + swap(block, axis, bit)
        bit *= 2
    return block


def source_col(row):
    return row * lax.axis_size("col") // lax.axis_size("row")


def blocks_to_send(blocks):
    rows, cols = lax.axis_size("row"), lax.axis_size("col")
    held = []
    for d in range(cols):
        wanted = [((r * cols + (source_col(r) ^ d)) % rows) ^ r for r in range(rows)]
        if len(set(wanted)) == 1:
            held.append(blocks[wanted[0]])
        else:
            held.append(lax.dynamic_index_in_dim(jnp.stack(blocks), jnp.array(wanted)[lax.axis_index("row")], 0, keepdims=False))
    return held


def spread_step(held):
    rows, cols = lax.axis_size("row"), lax.axis_size("col")
    bit = len(held) // 2
    pairs = [(r * cols + c, r * cols + (c ^ bit)) for r in range(rows) for c in range(cols)
             if (c ^ source_col(r)) % (2 * bit) == 0]
    moved = lax.ppermute(jnp.stack(held[bit:]), ("row", "col"), pairs)
    offset = lax.axis_index("col") ^ source_col(lax.axis_index("row"))
    return [jnp.where(offset & bit != 0, moved[j], held[j]) for j in range(bit)]


def own_output_rows_direct(block):
    rows, cols = lax.axis_size("row"), lax.axis_size("col")
    pairs = [(r * cols + c, c * rows + r) for r in range(rows) for c in range(cols)]
    return lax.ppermute(block, ("row", "col"), pairs)


def local(inverse_tile, panels, link_panel, diag_inverse, ancestor_tiles):
    rows_axis, cols_axis = lax.axis_size("row"), lax.axis_size("col")
    row_id, col_id = lax.axis_index("row"), lax.axis_index("col")
    siblings, _, local_rows, width = panels.shape
    height, span = diag_inverse.shape[2:]
    row_start = (col_id * rows_axis + row_id) * local_rows
    tile_mask = jnp.repeat(ancestor_tiles, TILE, axis=2)
    kept_rows = lax.dynamic_slice_in_dim(tile_mask, row_start, local_rows, 2).astype(jnp.float32)
    masked = panels * kept_rows[..., None]
    tiles = [half.reshape(cols_axis, -1, half.shape[1]) for half in split(inverse_tile)]

    def by_cols(*terms):
        terms = jnp.concatenate([term.reshape(width, cols_axis, span).swapaxes(0, 1) for term in terms], axis=2)
        return by_xor(terms, "col")

    def by_rows(terms):
        return by_xor(terms.reshape(rows_axis, height, -1), "row")

    def one_pair(first, panel_second, link, given_first, given_second):
        live = {"tiles": tiles, "first": first, "second": panel_second - dot(first, link, precise)}
        slots = {}

        def at(slot, *steps):
            slots.setdefault(slot, []).extend(steps)

        late = 2 * span
        pieces = [("first", i, i + late) for i in range(0, width, late)]
        count_first = len(pieces)
        pieces += [("second", i, i + late) for i in range(0, width - late, late)]
        count_early = len(pieces)
        pieces += [("second", i, i + span) for i in range(width - late, width, span)]
        stages = rows_axis.bit_length() - 1

        def fetch(k, stage):
            if stage == 0:
                panel, start, stop = pieces[k]
                live[k, 0] = live[panel][:, start:stop]
            for j in range(1, rows_axis):
                if j.bit_count() == stage + 1:
                    live[k, j] = swap(live[k, j & (j - 1)], "row", j & -j)

        def blocks(k):
            return [live[k, j] for j in range(rows_axis)]

        def multiply(k):
            live["send", k], live["keep", k] = product(live["tiles"], blocks(k))
            if k >= count_early:
                live["products", k] = jnp.concatenate([live["send", k], live["keep", k]]).reshape(-1, span)

        def add_core(k):
            live["sums", k] = live.pop(("keep", k)) + swap(live.pop(("send", k)), "col", 1)

        def add_rest(k):
            live["out", k] = -sum_scatter(live.pop(("sums", k)), "col", 2)

        def collect(name, start, stop):
            groups = zip(*(blocks(k) for k in range(start, stop)))
            live[name] = blocks_to_send([jnp.concatenate(group, axis=1) for group in groups])
            spread(name)
            for k in range(start, stop):
                for j in range(rows_axis):
                    del live[k, j]

        def spread(name):
            live[name] = spread_step(live[name])

        def own(name, slot, start, stop):
            at(slot, lambda: collect(name, start, stop))
            for step in range(1, cols_axis.bit_length() - 1):
                at(slot + step, lambda: spread(name))

        def outs(start, stop):
            return jnp.concatenate([live["out", k] for k in range(start, stop)], axis=1)

        for k in range(len(pieces)):
            for stage in range(stages):
                at(k + stage, lambda k=k, stage=stage: fetch(k, stage))

        def own_last():
            live["own_last"] = own_output_rows_direct(live["second"][:, width - late:])

        def given_link():
            link_cols = lax.dynamic_slice_in_dim(link, col_id * span, span, 1)
            given = {0: given_first}
            bit = cols_axis // 2
            while bit >= 1:
                given.update({j ^ bit: swap(block, "col", bit) for j, block in list(given.items())})
                bit //= 2
            given = [given[j].T for j in range(cols_axis)]
            live["given_link"] = dot_tn(placed(given, "col"), link_cols, precise)

        def first_terms():
            live["first_terms"] = sum_scatter(
                by_cols(dot_tn(live["own_first"][0], outs(0, count_first), three_pass)), "col")

        def first_sum():
            live["first_sum"] = sum_scatter(by_rows(live.pop("first_terms")), "row")

        def early_terms():
            out_early = outs(count_first, count_early)
            own_second = jnp.concatenate([live["own_early"][0], live["own_last"]], axis=1)
            cross = dot_tn(outs(0, count_first), own_second, three_pass)
            early = jnp.concatenate([
                dot_tn(own_second, out_early, three_pass),
                jnp.pad(dot_tn(out_early, live["own_last"], three_pass), ((0, late), (0, 0)))], axis=1)
            live["early_terms"] = sum_scatter(by_cols(cross, early), "col")

        def early_sum():
            link_rows = lax.dynamic_slice_in_dim(link, row_id * height, height, 0)
            terms = live.pop("early_terms")
            terms = terms.at[:, span:].add(-dot_tn(link_rows, live["given_link"], precise))
            live["early_sum"] = sum_scatter(by_rows(terms), "row")

        def own_last_rows(bit):
            rows = live.setdefault("last_rows", {0: live["own_last"]})
            rows.update({j ^ bit: swap(block, "col", bit) for j, block in list(rows.items())})
            if bit == 1:
                order = [*range(1, cols_axis, 2), *range(0, cols_axis, 2)]
                live["last_rows"] = jnp.concatenate([rows[j] for j in order])

        def last_terms(k):
            start = (k - count_early) * span
            terms = -dot_tn(live["last_rows"][:, start:], live["products", k], three_pass)
            count = cols_axis * terms.shape[1] // terms.shape[0]
            live["last", k] = sum_to_last(sum_to_last(terms, "col", count), "row", count)

        end = len(pieces) - 1 + stages
        for k in range(len(pieces)):
            at(k + stages, lambda k=k: multiply(k))
            if k >= count_early:
                at(end, lambda k=k: last_terms(k))
            at(min(k + stages + 1, end), lambda k=k: add_core(k))
            at(min(k + stages + 2, end), lambda k=k: add_rest(k))
            if k == 0:
                at(1, own_last)
                at(1, given_link)
                for step in range(cols_axis.bit_length() - 1):
                    at(2 + step, lambda bit=cols_axis >> (step + 1): own_last_rows(bit))
            if k == count_first - 1:
                own("own_first", k + stages, 0, count_first)
                at(k + stages + 2, first_terms)
                at(k + stages + 3, first_sum)
            if k == count_early - 1:
                own("own_early", k + stages, count_first, count_early)
                at(end, early_terms)
                at(end, early_sum)

        for slot in range(end + 1):
            if slot > 0:
                live = dict(zip(live, lax.optimization_barrier(list(live.values()))))
            for step in slots[slot]:
                step()

        last_a, last_b = live["last", end - stages - 1], live["last", end - stages]
        last = jnp.concatenate([last_a, jnp.concatenate([last_a[span:].T, last_b], axis=0)], axis=1)
        padded = jnp.pad(last, ((height, 0), (span, 0)))
        corner = width - late
        last_sum = lax.dynamic_slice(
            padded,
            (jnp.maximum(row_id * height - corner + height, 0), jnp.maximum(col_id * span - corner + span, 0)),
            (height, span))
        cross_sum, early = live["early_sum"][:, :span], live["early_sum"][:, span:]
        ancestor = jnp.stack([outs(0, count_first), outs(count_first, len(pieces))])
        diagonal = jnp.stack([given_first - live["first_sum"], given_second - early - last_sum])
        return ancestor, diagonal, -(cross_sum + live["given_link"])

    results = [one_pair(masked[s, 0], masked[s, 1], link_panel[s], diag_inverse[s, 0], diag_inverse[s, 1])
               for s in range(siblings)]
    return tuple(jnp.stack(group) for group in zip(*results))


def solution(mesh):
    in_specs = (
        P(("hyp", "row"), "col"),
        P("hyp", None, ("col", "row"), None),
        P("hyp", None, None),
        P("hyp", None, "row", "col"),
        P(),
    )
    out_specs = (
        P("hyp", None, ("row", "col"), None),
        P("hyp", None, "row", "col"),
        P("hyp", "row", "col"),
    )
    return jax.shard_map(local, mesh=mesh, in_specs=in_specs, out_specs=out_specs, check_vma=False)
```

```python
import jax
import jax.numpy as jnp
from jax import lax
from jax.experimental import pallas as pl
from jax.experimental.pallas import tpu as pltpu
from jax.sharding import PartitionSpec as P

TILE = 128

precise = lax.Precision.HIGHEST
three_pass = lax.Precision.HIGH


def swap(block, axis, bit):
    pairs = [(i, i ^ bit) for i in range(lax.axis_size(axis))]
    return lax.ppermute(block, axis, pairs)


def parts(values):
    high = values.astype(jnp.bfloat16)
    return high, (values - high.astype(jnp.float32)).astype(jnp.bfloat16)


def split_kernel(tile_ref, high_ref, low_ref):
    high_ref[...], low_ref[...] = parts(tile_ref[...])


def split(tile):
    rows, width = tile.shape
    step = min(rows, 256)
    block = pl.BlockSpec((step, width), lambda t: (t, 0))
    return pl.pallas_call(
        split_kernel,
        grid=(rows // step,),
        in_specs=[block],
        out_specs=[block, block],
        out_shape=[jax.ShapeDtypeStruct(tile.shape, jnp.bfloat16)] * 2,
        compiler_params=pltpu.CompilerParams(vmem_limit_bytes=40 * 2**20),
    )(tile)


def product_kernel(place, tile_high_ref, tile_low_ref, *refs):
    *block_refs, send_ref, keep_ref, high_ref, low_ref = refs
    height = block_refs[0].shape[0]
    half = send_ref.shape[0]
    for j, block_ref in enumerate(block_refs):
        rows = pl.ds(pl.multiple_of((place[0] ^ j) * height, height), height)
        high_ref[rows], low_ref[rows] = parts(block_ref[...])

    def times(a, b_ref):
        return jnp.dot(a, b_ref[...], preferred_element_type=jnp.float32)

    for first, out_ref in ((1, send_ref), (1 + half, keep_ref)):
        def step(i, carry):
            chunk = place[first + i]
            high, low = tile_high_ref[chunk], tile_low_ref[chunk]
            out_ref[i] = times(high, high_ref) + (times(high, low_ref) + times(low, high_ref))
            return carry

        lax.fori_loop(0, half, step, 0)


def product(tiles, blocks):
    count, out_rows, width = tiles[0].shape
    columns = blocks[0].shape[1]
    half = count // 2
    chunks = lax.axis_index("col") ^ jnp.concatenate([2 * jnp.arange(half) + 1, 2 * jnp.arange(half)])
    place = jnp.concatenate([lax.axis_index("row")[None], chunks]).astype(jnp.int32)
    vmem = pl.BlockSpec(memory_space=pltpu.VMEM)
    return pl.pallas_call(
        product_kernel,
        in_specs=[pl.BlockSpec(memory_space=pltpu.SMEM)] + [vmem] * (2 + len(blocks)),
        out_specs=[vmem, vmem],
        out_shape=[jax.ShapeDtypeStruct((half, out_rows, columns), jnp.float32)] * 2,
        scratch_shapes=[pltpu.VMEM((width, columns), jnp.bfloat16)] * 2,
        compiler_params=pltpu.CompilerParams(vmem_limit_bytes=40 * 2**20),
    )(place, *tiles, *blocks)


def dot(a, b, precision):
    return jnp.matmul(a, b, precision=precision)


def dot_tn(a, b, precision):
    return lax.dot_general(a, b, (((0,), (0,)), ((), ())), precision=precision)


def sum_scatter(blocks, axis, bit=1):
    while blocks.shape[0] > 1:
        pairs = blocks.reshape((blocks.shape[0] // 2, 2) + blocks.shape[1:])
        blocks = pairs[:, 0] + swap(pairs[:, 1], axis, bit)
        bit *= 2
    return blocks[0]


def sum_rows(blocks, axis):
    bit = 1
    while blocks.shape[0] > 1:
        mine = lax.axis_index(axis) // bit % 2
        pairs = blocks.reshape((blocks.shape[0] // 2, 2) + blocks.shape[1:])
        keep = lax.dynamic_index_in_dim(pairs, mine, 1, keepdims=False)
        blocks = keep + swap(lax.dynamic_index_in_dim(pairs, 1 - mine, 1, keepdims=False), axis, bit)
        bit *= 2
    return blocks[0]


def columns_by_xor(array, odd):
    cols, col_id = lax.axis_size("col"), lax.axis_index("col")
    span = array.shape[1] // cols
    return [lax.dynamic_slice_in_dim(array, (col_id ^ j) * span, span, 1) for j in range(odd, cols, 2)]


def source_col(row):
    return row * lax.axis_size("col") // lax.axis_size("row")


def blocks_to_send(blocks):
    rows, cols = lax.axis_size("row"), lax.axis_size("col")
    held = []
    for d in range(cols):
        wanted = [((r * cols + (source_col(r) ^ d)) % rows) ^ r for r in range(rows)]
        if len(set(wanted)) == 1:
            held.append(blocks[wanted[0]])
        else:
            held.append(lax.dynamic_index_in_dim(jnp.stack(blocks), jnp.array(wanted)[lax.axis_index("row")], 0, keepdims=False))
    return held


def spread_step(held):
    rows, cols = lax.axis_size("row"), lax.axis_size("col")
    bit = len(held) // 2
    pairs = [(r * cols + c, r * cols + (c ^ bit)) for r in range(rows) for c in range(cols)
             if (c ^ source_col(r)) % (2 * bit) == 0]
    moved = lax.ppermute(jnp.stack(held[bit:]), ("row", "col"), pairs)
    offset = lax.axis_index("col") ^ source_col(lax.axis_index("row"))
    return [jnp.where(offset & bit != 0, moved[j], held[j]) for j in range(bit)]


def local(inverse_tile, panels, link_panel, diag_inverse, ancestor_tiles):
    rows_axis, cols_axis = lax.axis_size("row"), lax.axis_size("col")
    row_id, col_id = lax.axis_index("row"), lax.axis_index("col")
    siblings, _, local_rows, width = panels.shape
    height, span = diag_inverse.shape[2:]
    row_start = (col_id * rows_axis + row_id) * local_rows
    tile_mask = jnp.repeat(ancestor_tiles, TILE, axis=2)
    kept_rows = lax.dynamic_slice_in_dim(tile_mask, row_start, local_rows, 2).astype(jnp.float32)
    masked = panels * kept_rows[..., None]
    tiles = [half.reshape(cols_axis, -1, half.shape[1]) for half in split(inverse_tile)]

    def one_pair(first, panel_second, link, given_first, given_second):
        live = {"tiles": tiles, "given": given_first, "first": first, "second": panel_second - dot(first, link, precise)}
        slots = {}

        def at(slot, *steps):
            slots.setdefault(slot, []).extend(steps)

        late = 2 * span
        pieces = [("first", i, i + late) for i in range(0, width, late)]
        count_first = len(pieces)
        pieces += [("second", i, i + late) for i in range(0, width, late)]
        count_early = len(pieces) - 1
        stages = rows_axis.bit_length() - 1

        def fetch(k, stage):
            if stage == 0:
                panel, start, stop = pieces[k]
                live[k, 0] = live[panel][:, start:stop]
            for j in range(1, rows_axis):
                if j.bit_count() == stage + 1:
                    live[k, j] = swap(live[k, j & (j - 1)], "row", j & -j)

        def blocks(k):
            return [live[k, j] for j in range(rows_axis)]

        def multiply(k):
            live["send", k], live["keep", k] = product(live["tiles"], blocks(k))

        def add_core(k):
            live["sums", k] = live.pop(("keep", k)) + swap(live.pop(("send", k)), "col", 1)

        def add_rest(k):
            live["out", k] = -sum_scatter(live.pop(("sums", k)), "col", 2)

        def collect(name, start, stop):
            groups = zip(*(blocks(k) for k in range(start, stop)))
            live[name] = blocks_to_send([jnp.concatenate(group, axis=1) for group in groups])
            spread(name)
            for k in range(start, stop):
                for j in range(rows_axis):
                    del live[k, j]

        def spread(name):
            live[name] = spread_step(live[name])

        def own(name, slot, start, stop):
            at(slot, lambda: collect(name, start, stop))
            for step in range(1, cols_axis.bit_length() - 1):
                at(slot + step, lambda: spread(name))

        def outs(start, stop):
            return jnp.concatenate([live["out", k] for k in range(start, stop)], axis=1)

        for k in range(len(pieces)):
            for stage in range(stages):
                at(k + stage, lambda k=k, stage=stage: fetch(k, stage))

        def link_terms():
            link_rows = lax.dynamic_slice_in_dim(link, row_id * height, height, 0)
            link_cols = lax.dynamic_slice_in_dim(link, col_id * span, span, 0)
            given = dot(live["given"], link_cols, precise)
            live["link_cross"] = lax.dynamic_update_slice_in_dim(jnp.zeros_like(link), given, row_id * height, 0)
            live["link_second"] = -dot_tn(link_rows, given, precise)

        def own_second():
            return jnp.concatenate([live["own_early"][0], live["own_last"][0]], axis=1)

        def first_terms():
            out_first = outs(0, count_first)
            terms = jnp.stack([dot_tn(out_first, live["own_first"][0], three_pass),
                               dot_tn(out_first, own_second(), three_pass) + live["link_cross"]])
            terms = terms.reshape(2 * width, cols_axis, span).swapaxes(0, 1)
            terms = lax.psum_scatter(terms, "col", scatter_dimension=0)
            terms = terms.reshape(2, rows_axis, height, span).swapaxes(0, 1)
            live["first_sums"] = lax.psum_scatter(terms, "row", scatter_dimension=0)

        def second_terms():
            out_second = outs(count_first, len(pieces))

            def terms(odd):
                own_columns, link_columns = (jnp.concatenate(columns_by_xor(array, odd), axis=1)
                                             for array in (own_second(), live["link_second"]))
                return dot_tn(out_second, own_columns, three_pass) + link_columns

            sent = swap(terms(1), "col", 1)
            sums = (terms(0) + sent).reshape(width, cols_axis // 2, span).swapaxes(0, 1)
            sums = sum_scatter(sums, "col", 2)
            live["second_sum"] = sum_rows(sums.reshape(rows_axis, height, span), "row")

        end = len(pieces) - 1 + stages
        for k in range(len(pieces)):
            at(k + stages, lambda k=k: multiply(k))
            at(min(k + stages + 1, end), lambda k=k: add_core(k))
            at(min(k + stages + 1, end), lambda k=k: add_rest(k))
            if k == 0:
                at(1, link_terms)
            if k == count_first - 1:
                own("own_first", k + stages, 0, count_first)
            if k == count_early - 1:
                own("own_early", k + stages, count_first, count_early)
        at(end, lambda: collect("own_last", count_early, len(pieces)))
        for step in range(1, cols_axis.bit_length() - 1):
            at(end, lambda: spread("own_last"))
        at(end, first_terms)
        at(end, second_terms)

        for slot in range(end + 1):
            if slot > 0:
                live = dict(zip(live, lax.optimization_barrier(list(live.values()))))
            for step in slots[slot]:
                step()

        first_sum, cross_sum = live["first_sums"]
        ancestor = jnp.stack([outs(0, count_first), outs(count_first, len(pieces))])
        diagonal = jnp.stack([given_first - first_sum, given_second - live["second_sum"]])
        return ancestor, diagonal, -cross_sum

    results = [one_pair(masked[s, 0], masked[s, 1], link_panel[s], diag_inverse[s, 0], diag_inverse[s, 1])
               for s in range(siblings)]
    return tuple(jnp.stack(group) for group in zip(*results))


def solution(mesh):
    in_specs = (
        P(("hyp", "row"), "col"),
        P("hyp", None, ("col", "row"), None),
        P("hyp", None, None),
        P("hyp", None, "row", "col"),
        P(),
    )
    out_specs = (
        P("hyp", None, ("row", "col"), None),
        P("hyp", None, "row", "col"),
        P("hyp", "row", "col"),
    )
    return jax.shard_map(local, mesh=mesh, in_specs=in_specs, out_specs=out_specs, check_vma=False)
```

```python
import jax
import jax.numpy as jnp
from jax import lax
from jax.experimental import pallas as pl
from jax.experimental.pallas import tpu as pltpu
from jax.sharding import PartitionSpec as P

TILE = 128

precise = lax.Precision.HIGHEST
three_pass = lax.Precision.HIGH


def swap(block, axis, bit):
    pairs = [(i, i ^ bit) for i in range(lax.axis_size(axis))]
    return lax.ppermute(block, axis, pairs)


def parts(values):
    high = values.astype(jnp.bfloat16)
    return high, (values - high.astype(jnp.float32)).astype(jnp.bfloat16)


def split_kernel(tile_ref, high_ref, low_ref):
    high_ref[...], low_ref[...] = parts(tile_ref[...])


def split(tile):
    rows, width = tile.shape
    step = min(rows, 256)
    block = pl.BlockSpec((step, width), lambda t: (t, 0))
    return pl.pallas_call(
        split_kernel,
        grid=(rows // step,),
        in_specs=[block],
        out_specs=[block, block],
        out_shape=[jax.ShapeDtypeStruct(tile.shape, jnp.bfloat16)] * 2,
        compiler_params=pltpu.CompilerParams(vmem_limit_bytes=16 * 2**20),
    )(tile)


def product_kernel(place, tile_high_ref, tile_low_ref, *refs):
    *block_refs, send_ref, keep_ref, high_ref, low_ref = refs
    height = block_refs[0].shape[0]
    half = send_ref.shape[0]
    for j, block_ref in enumerate(block_refs):
        rows = pl.ds(pl.multiple_of((place[0] ^ j) * height, height), height)
        high_ref[rows], low_ref[rows] = parts(block_ref[...])

    def times(a, b_ref):
        return jnp.dot(a, b_ref[...], preferred_element_type=jnp.float32)

    for first, out_ref in ((1, send_ref), (1 + half, keep_ref)):
        def step(i, carry):
            chunk = place[first + i]
            high, low = tile_high_ref[chunk], tile_low_ref[chunk]
            out_ref[i] = times(high, high_ref) + (times(high, low_ref) + times(low, high_ref))
            return carry

        lax.fori_loop(0, half, step, 0)


def product(tiles, blocks):
    count, out_rows, width = tiles[0].shape
    columns = blocks[0].shape[1]
    half = count // 2
    chunks = lax.axis_index("col") ^ jnp.concatenate([2 * jnp.arange(half) + 1, 2 * jnp.arange(half)])
    place = jnp.concatenate([lax.axis_index("row")[None], chunks]).astype(jnp.int32)
    vmem = pl.BlockSpec(memory_space=pltpu.VMEM)
    return pl.pallas_call(
        product_kernel,
        in_specs=[pl.BlockSpec(memory_space=pltpu.SMEM)] + [vmem] * (2 + len(blocks)),
        out_specs=[vmem, vmem],
        out_shape=[jax.ShapeDtypeStruct((half, out_rows, columns), jnp.float32)] * 2,
        scratch_shapes=[pltpu.VMEM((width, columns), jnp.bfloat16)] * 2,
        compiler_params=pltpu.CompilerParams(vmem_limit_bytes=16 * 2**20),
    )(place, *tiles, *blocks)


def dot(a, b, precision):
    return jnp.matmul(a, b, precision=precision)


def dot_tn(a, b, precision):
    return lax.dot_general(a, b, (((0,), (0,)), ((), ())), precision=precision)


def sum_scatter(blocks, axis, bit=1):
    while blocks.shape[0] > 1:
        pairs = blocks.reshape((blocks.shape[0] // 2, 2) + blocks.shape[1:])
        blocks = pairs[:, 0] + swap(pairs[:, 1], axis, bit)
        bit *= 2
    return blocks[0]


def sum_rows(blocks, axis):
    bit = 1
    while blocks.shape[0] > 1:
        mine = lax.axis_index(axis) // bit % 2
        pairs = blocks.reshape((blocks.shape[0] // 2, 2) + blocks.shape[1:])
        keep = lax.dynamic_index_in_dim(pairs, mine, 1, keepdims=False)
        blocks = keep + swap(lax.dynamic_index_in_dim(pairs, 1 - mine, 1, keepdims=False), axis, bit)
        bit *= 2
    return blocks[0]


def columns_by_xor(array, odd):
    cols, col_id = lax.axis_size("col"), lax.axis_index("col")
    span = array.shape[1] // cols
    return [lax.dynamic_slice_in_dim(array, (col_id ^ j) * span, span, 1) for j in range(odd, cols, 2)]


def source_col(row):
    return row * lax.axis_size("col") // lax.axis_size("row")


def blocks_to_send(blocks):
    rows, cols = lax.axis_size("row"), lax.axis_size("col")
    held = []
    for d in range(cols):
        wanted = [((r * cols + (source_col(r) ^ d)) % rows) ^ r for r in range(rows)]
        if len(set(wanted)) == 1:
            held.append(blocks[wanted[0]])
        else:
            held.append(lax.dynamic_index_in_dim(jnp.stack(blocks), jnp.array(wanted)[lax.axis_index("row")], 0, keepdims=False))
    return held


def spread_step(held):
    rows, cols = lax.axis_size("row"), lax.axis_size("col")
    bit = len(held) // 2
    pairs = [(r * cols + c, r * cols + (c ^ bit)) for r in range(rows) for c in range(cols)
             if (c ^ source_col(r)) % (2 * bit) == 0]
    moved = lax.ppermute(jnp.stack(held[bit:]), ("row", "col"), pairs)
    offset = lax.axis_index("col") ^ source_col(lax.axis_index("row"))
    return [jnp.where(offset & bit != 0, moved[j], held[j]) for j in range(bit)]


def local(inverse_tile, panels, link_panel, diag_inverse, ancestor_tiles):
    rows_axis, cols_axis = lax.axis_size("row"), lax.axis_size("col")
    row_id, col_id = lax.axis_index("row"), lax.axis_index("col")
    siblings, _, local_rows, width = panels.shape
    height, span = diag_inverse.shape[2:]
    row_start = (col_id * rows_axis + row_id) * local_rows
    tile_mask = jnp.repeat(ancestor_tiles, TILE, axis=2)
    kept_rows = lax.dynamic_slice_in_dim(tile_mask, row_start, local_rows, 2).astype(jnp.float32)
    masked = panels * kept_rows[..., None]
    tiles = [half.reshape(cols_axis, -1, half.shape[1]) for half in split(inverse_tile)]

    def one_pair(first, panel_second, link, given_first, given_second):
        live = {"tiles": tiles, "given": given_first, "first": first, "second": panel_second - dot(first, link, precise)}
        slots = {}

        def at(slot, *steps):
            slots.setdefault(slot, []).extend(steps)

        late = 2 * span
        pieces = [("first", i, i + late) for i in range(0, width, late)]
        count_first = len(pieces)
        pieces += [("second", i, i + late) for i in range(0, width, late)]
        stages = rows_axis.bit_length() - 1

        def fetch(k, stage):
            if stage == 0:
                panel, start, stop = pieces[k]
                live[k, 0] = live[panel][:, start:stop]
            for j in range(1, rows_axis):
                if j.bit_count() == stage + 1:
                    live[k, j] = swap(live[k, j & (j - 1)], "row", j & -j)

        def blocks(k):
            return [live[k, j] for j in range(rows_axis)]

        def multiply(k):
            live["send", k], live["keep", k] = product(live["tiles"], blocks(k))

        def add_core(k):
            live["sums", k] = live.pop(("keep", k)) + swap(live.pop(("send", k)), "col", 1)

        def add_rest(k):
            live["out", k] = -sum_scatter(live.pop(("sums", k)), "col", 2)

        def collect(k):
            live["own", k] = blocks_to_send(blocks(k))
            spread(k)

        def spread(k):
            live["own", k] = spread_step(live["own", k])

        def owns(start, stop):
            return jnp.concatenate([live["own", k][0] for k in range(start, stop)], axis=1)

        def outs(start, stop):
            return jnp.concatenate([live["out", k] for k in range(start, stop)], axis=1)

        for k in range(len(pieces)):
            for stage in range(stages):
                at(k + stage, lambda k=k, stage=stage: fetch(k, stage))

        def link_terms():
            link_rows = lax.dynamic_slice_in_dim(link, row_id * height, height, 0)
            link_cols = lax.dynamic_slice_in_dim(link, col_id * span, span, 0)
            given = dot(live["given"], link_cols, precise)
            live["link_cross"] = lax.dynamic_update_slice_in_dim(jnp.zeros_like(link), given, row_id * height, 0)
            live["link_second"] = -dot_tn(link_rows, given, precise)

        def core_sum(terms):
            sent = swap(terms(1), "col", 1)
            return terms(0) + sent

        def spread_sum(sums):
            sums = sums.reshape(-1, cols_axis // 2, span).swapaxes(0, 1)
            sums = sum_scatter(sums, "col", 2)
            return sum_rows(sums.reshape(-1, rows_axis, height, span).swapaxes(0, 1), "row")

        def by_parity(array, odd):
            return jnp.concatenate(columns_by_xor(array, odd), axis=1)

        def first_terms():
            out_first = outs(0, count_first)
            own_first, own_second = owns(0, count_first), owns(count_first, len(pieces))

            def terms(odd):
                cross = dot_tn(out_first, by_parity(own_second, odd), three_pass) + by_parity(live["link_cross"], odd)
                return jnp.concatenate([dot_tn(out_first, by_parity(own_first, odd), three_pass), cross])

            live["first_sums"] = core_sum(terms)

        def first_sums():
            live["first_sums"] = spread_sum(live["first_sums"])

        def second_terms():
            out_second, own_second = outs(count_first, len(pieces)), owns(count_first, len(pieces))

            def terms(odd):
                return dot_tn(out_second, by_parity(own_second, odd), three_pass) + by_parity(live["link_second"], odd)

            live["second_sum"] = spread_sum(core_sum(terms))[0]

        at(1, link_terms)
        for k in range(len(pieces)):
            at(k + stages, lambda k=k: collect(k), lambda k=k: multiply(k))
            for step in range(1, cols_axis.bit_length() - 1):
                at(k + stages + step, lambda k=k: spread(k))
            at(k + stages + 1, lambda k=k: add_core(k))
            at(k + stages + (2 if k + 1 < len(pieces) else 1), lambda k=k: add_rest(k))
        end = len(pieces) + stages + 1
        at(end - 1, first_terms)
        at(end, first_sums, second_terms)

        for slot in range(end + 1):
            if slot > 0:
                live = dict(zip(live, lax.optimization_barrier(list(live.values()))))
            for step in slots[slot]:
                step()

        first_sum, cross_sum = live["first_sums"]
        ancestor = jnp.stack([outs(0, count_first), outs(count_first, len(pieces))])
        diagonal = jnp.stack([given_first - first_sum, given_second - live["second_sum"]])
        return ancestor, diagonal, -cross_sum

    results = [one_pair(masked[s, 0], masked[s, 1], link_panel[s], diag_inverse[s, 0], diag_inverse[s, 1])
               for s in range(siblings)]
    return tuple(jnp.stack(group) for group in zip(*results))


def solution(mesh):
    in_specs = (
        P(("hyp", "row"), "col"),
        P("hyp", None, ("col", "row"), None),
        P("hyp", None, None),
        P("hyp", None, "row", "col"),
        P(),
    )
    out_specs = (
        P("hyp", None, ("row", "col"), None),
        P("hyp", None, "row", "col"),
        P("hyp", "row", "col"),
    )
    return jax.shard_map(local, mesh=mesh, in_specs=in_specs, out_specs=out_specs, check_vma=False)
```

```python
import jax
import jax.numpy as jnp
from jax import lax
from jax.experimental import pallas as pl
from jax.experimental.pallas import tpu as pltpu
from jax.sharding import PartitionSpec as P

TILE = 128

precise = lax.Precision.HIGHEST
three_pass = lax.Precision.HIGH


def swap(block, axis, bit):
    pairs = [(i, i ^ bit) for i in range(lax.axis_size(axis))]
    return lax.ppermute(block, axis, pairs)


def parts(values):
    high = values.astype(jnp.bfloat16)
    return high, (values - high.astype(jnp.float32)).astype(jnp.bfloat16)


def split_kernel(tile_ref, high_ref, low_ref, held, arrived):
    step = held.shape[1]

    def fetch(t):
        return pltpu.make_async_copy(tile_ref.at[pl.ds(t * step, step)], held.at[t % 2], arrived.at[t % 2])

    count = tile_ref.shape[0] // step
    fetch(0).start()
    for t in range(count):
        if t + 1 < count:
            fetch(t + 1).start()
        fetch(t).wait()
        rows = pl.ds(t * step, step)
        high_ref[rows], low_ref[rows] = parts(held[t % 2])


def split(tile):
    rows, width = tile.shape
    step = min(rows, 256)
    return pl.pallas_call(
        split_kernel,
        in_specs=[pl.BlockSpec(memory_space=pltpu.HBM)],
        out_specs=[pl.BlockSpec(memory_space=pltpu.VMEM)] * 2,
        out_shape=[jax.ShapeDtypeStruct(tile.shape, jnp.bfloat16)] * 2,
        scratch_shapes=[pltpu.VMEM((2, step, width), jnp.float32), pltpu.SemaphoreType.DMA((2,))],
        compiler_params=pltpu.CompilerParams(vmem_limit_bytes=16 * 2**20),
    )(tile)


def product_kernel(place, tile_high_ref, tile_low_ref, *refs):
    *block_refs, send_ref, keep_ref, high_ref, low_ref = refs
    height = block_refs[0].shape[0]
    half = send_ref.shape[0]
    for j, block_ref in enumerate(block_refs):
        rows = pl.ds(pl.multiple_of((place[0] ^ j) * height, height), height)
        high_ref[rows], low_ref[rows] = parts(block_ref[...])

    def times(a, b_ref):
        return jnp.dot(a, b_ref[...], preferred_element_type=jnp.float32)

    for first, out_ref in ((1, send_ref), (1 + half, keep_ref)):
        def step(i, carry):
            chunk = place[first + i]
            high, low = tile_high_ref[chunk], tile_low_ref[chunk]
            out_ref[i] = times(high, high_ref) + (times(high, low_ref) + times(low, high_ref))
            return carry

        lax.fori_loop(0, half, step, 0)


def product(tiles, blocks):
    count, out_rows, width = tiles[0].shape
    columns = blocks[0].shape[1]
    half = count // 2
    chunks = lax.axis_index("col") ^ jnp.concatenate([2 * jnp.arange(half) + 1, 2 * jnp.arange(half)])
    place = jnp.concatenate([lax.axis_index("row")[None], chunks]).astype(jnp.int32)
    vmem = pl.BlockSpec(memory_space=pltpu.VMEM)
    return pl.pallas_call(
        product_kernel,
        in_specs=[pl.BlockSpec(memory_space=pltpu.SMEM)] + [vmem] * (2 + len(blocks)),
        out_specs=[vmem, vmem],
        out_shape=[jax.ShapeDtypeStruct((half, out_rows, columns), jnp.float32)] * 2,
        scratch_shapes=[pltpu.VMEM((width, columns), jnp.bfloat16)] * 2,
        compiler_params=pltpu.CompilerParams(vmem_limit_bytes=16 * 2**20),
    )(place, *tiles, *blocks)


def dot(a, b, precision):
    return jnp.matmul(a, b, precision=precision)


def dot_tn(a, b, precision):
    return lax.dot_general(a, b, (((0,), (0,)), ((), ())), precision=precision)


def sum_scatter(blocks, axis, bit=1):
    while blocks.shape[0] > 1:
        pairs = blocks.reshape((blocks.shape[0] // 2, 2) + blocks.shape[1:])
        blocks = pairs[:, 0] + swap(pairs[:, 1], axis, bit)
        bit *= 2
    return blocks[0]


def sum_rows(blocks, axis):
    bit = 1
    while blocks.shape[0] > 1:
        mine = lax.axis_index(axis) // bit % 2
        pairs = blocks.reshape((blocks.shape[0] // 2, 2) + blocks.shape[1:])
        keep = lax.dynamic_index_in_dim(pairs, mine, 1, keepdims=False)
        blocks = keep + swap(lax.dynamic_index_in_dim(pairs, 1 - mine, 1, keepdims=False), axis, bit)
        bit *= 2
    return blocks[0]


def columns_by_xor(array, odd):
    cols, col_id = lax.axis_size("col"), lax.axis_index("col")
    span = array.shape[1] // cols
    return [lax.dynamic_slice_in_dim(array, (col_id ^ j) * span, span, 1) for j in range(odd, cols, 2)]


def source_col(row):
    return row * lax.axis_size("col") // lax.axis_size("row")


def blocks_to_send(blocks):
    rows, cols = lax.axis_size("row"), lax.axis_size("col")
    held = []
    for d in range(cols):
        wanted = [((r * cols + (source_col(r) ^ d)) % rows) ^ r for r in range(rows)]
        if len(set(wanted)) == 1:
            held.append(blocks[wanted[0]])
        else:
            held.append(lax.dynamic_index_in_dim(jnp.stack(blocks), jnp.array(wanted)[lax.axis_index("row")], 0, keepdims=False))
    return held


def spread_step(held):
    rows, cols = lax.axis_size("row"), lax.axis_size("col")
    bit = len(held) // 2
    pairs = [(r * cols + c, r * cols + (c ^ bit)) for r in range(rows) for c in range(cols)
             if (c ^ source_col(r)) % (2 * bit) == 0]
    moved = lax.ppermute(jnp.stack(held[bit:]), ("row", "col"), pairs)
    offset = lax.axis_index("col") ^ source_col(lax.axis_index("row"))
    return [jnp.where(offset & bit != 0, moved[j], held[j]) for j in range(bit)]


def local(inverse_tile, panels, link_panel, diag_inverse, ancestor_tiles):
    rows_axis, cols_axis = lax.axis_size("row"), lax.axis_size("col")
    row_id, col_id = lax.axis_index("row"), lax.axis_index("col")
    siblings, _, local_rows, width = panels.shape
    height, span = diag_inverse.shape[2:]
    row_start = (col_id * rows_axis + row_id) * local_rows
    tile_mask = jnp.repeat(ancestor_tiles, TILE, axis=2)
    kept_rows = lax.dynamic_slice_in_dim(tile_mask, row_start, local_rows, 2).astype(jnp.float32)
    masked = panels * kept_rows[..., None]
    tiles = [half.reshape(cols_axis, -1, half.shape[1]) for half in split(inverse_tile)]

    def one_pair(first, panel_second, link, given_first, given_second):
        live = {"tiles": tiles, "given": given_first, "first": first, "second": panel_second - dot(first, link, precise)}
        slots = {}

        def at(slot, *steps):
            slots.setdefault(slot, []).extend(steps)

        late = 2 * span
        pieces = [("first", i, i + late) for i in range(0, width, late)]
        count_first = len(pieces)
        pieces += [("second", i, i + late) for i in range(0, width, late)]
        stages = rows_axis.bit_length() - 1

        def fetch(k, stage):
            if stage == 0:
                panel, start, stop = pieces[k]
                live[k, 0] = live[panel][:, start:stop]
            for j in range(1, rows_axis):
                if j.bit_count() == stage + 1:
                    live[k, j] = swap(live[k, j & (j - 1)], "row", j & -j)

        def blocks(k):
            return [live[k, j] for j in range(rows_axis)]

        def multiply(k):
            if "tiles" in live:
                tiles[:] = live.pop("tiles")
            live["send", k], live["keep", k] = product(tiles, blocks(k))

        def add_core(k):
            live["sums", k] = live.pop(("keep", k)) + swap(live.pop(("send", k)), "col", 1)

        def add_rest(k):
            live["out", k] = -sum_scatter(live.pop(("sums", k)), "col", 2)

        def collect(k):
            live["own", k] = blocks_to_send(blocks(k))
            spread(k)

        def spread(k):
            live["own", k] = spread_step(live["own", k])

        def owns(start, stop):
            return jnp.concatenate([live["own", k][0] for k in range(start, stop)], axis=1)

        def outs(start, stop):
            return jnp.concatenate([live["out", k] for k in range(start, stop)], axis=1)

        for k in range(len(pieces)):
            for stage in range(stages):
                at(k + stage, lambda k=k, stage=stage: fetch(k, stage))

        def link_terms():
            link_rows = lax.dynamic_slice_in_dim(link, row_id * height, height, 0)
            link_cols = lax.dynamic_slice_in_dim(link, col_id * span, span, 0)
            given = dot(live["given"], link_cols, precise)
            live["link_cross"] = lax.dynamic_update_slice_in_dim(jnp.zeros_like(link), given, row_id * height, 0)
            live["link_second"] = -dot_tn(link_rows, given, precise)

        def core_sum(terms):
            sent = swap(terms(1), "col", 1)
            return terms(0) + sent

        def spread_sum(sums):
            sums = sums.reshape(-1, cols_axis // 2, span).swapaxes(0, 1)
            sums = sum_scatter(sums, "col", 2)
            return sum_rows(sums.reshape(-1, rows_axis, height, span).swapaxes(0, 1), "row")

        def by_parity(array, odd):
            return jnp.concatenate(columns_by_xor(array, odd), axis=1)

        def first_terms():
            out_first = outs(0, count_first)
            own_first, own_second = owns(0, count_first), owns(count_first, len(pieces))

            def terms(odd):
                cross = dot_tn(out_first, by_parity(own_second, odd), three_pass) + by_parity(live["link_cross"], odd)
                return jnp.concatenate([dot_tn(out_first, by_parity(own_first, odd), three_pass), cross])

            live["first_sums"] = core_sum(terms)

        def first_sums():
            live["first_sums"] = spread_sum(live["first_sums"])

        def second_terms():
            out_second, own_second = outs(count_first, len(pieces)), owns(count_first, len(pieces))

            def terms(odd):
                return dot_tn(out_second, by_parity(own_second, odd), three_pass) + by_parity(live["link_second"], odd)

            live["second_sum"] = spread_sum(core_sum(terms))[0]

        at(1, link_terms)
        for k in range(len(pieces)):
            at(k + stages, lambda k=k: collect(k), lambda k=k: multiply(k))
            for step in range(1, cols_axis.bit_length() - 1):
                at(k + stages + step, lambda k=k: spread(k))
            at(k + stages + 1, lambda k=k: add_core(k))
            at(k + stages + 1, lambda k=k: add_rest(k))
        end = len(pieces) + stages + 1
        at(end - 1, first_terms)
        at(end, first_sums, second_terms)

        for slot in range(end + 1):
            if slot > 0:
                live = dict(zip(live, lax.optimization_barrier(list(live.values()))))
            for step in slots[slot]:
                step()

        first_sum, cross_sum = live["first_sums"]
        ancestor = jnp.stack([outs(0, count_first), outs(count_first, len(pieces))])
        diagonal = jnp.stack([given_first - first_sum, given_second - live["second_sum"]])
        return ancestor, diagonal, -cross_sum

    results = [one_pair(masked[s, 0], masked[s, 1], link_panel[s], diag_inverse[s, 0], diag_inverse[s, 1])
               for s in range(siblings)]
    return tuple(jnp.stack(group) for group in zip(*results))


def solution(mesh):
    in_specs = (
        P(("hyp", "row"), "col"),
        P("hyp", None, ("col", "row"), None),
        P("hyp", None, None),
        P("hyp", None, "row", "col"),
        P(),
    )
    out_specs = (
        P("hyp", None, ("row", "col"), None),
        P("hyp", None, "row", "col"),
        P("hyp", "row", "col"),
    )
    return jax.shard_map(local, mesh=mesh, in_specs=in_specs, out_specs=out_specs, check_vma=False)
```

```python
import jax
import jax.numpy as jnp
from jax import lax
from jax.experimental import pallas as pl
from jax.experimental.pallas import tpu as pltpu
from jax.sharding import PartitionSpec as P

TILE = 128

precise = lax.Precision.HIGHEST
three_pass = lax.Precision.HIGH


def swap(block, axis, bit):
    pairs = [(i, i ^ bit) for i in range(lax.axis_size(axis))]
    return lax.ppermute(block, axis, pairs)


def parts(values):
    high = values.astype(jnp.bfloat16)
    return high, (values - high.astype(jnp.float32)).astype(jnp.bfloat16)


def split_kernel(tile_ref, high_ref, low_ref):
    high_ref[...], low_ref[...] = parts(tile_ref[...])


def split(tile):
    rows, width = tile.shape
    step = min(rows, 256)
    block = pl.BlockSpec((step, width), lambda t: (t, 0))
    return pl.pallas_call(
        split_kernel,
        grid=(rows // step,),
        in_specs=[block],
        out_specs=[block, block],
        out_shape=[jax.ShapeDtypeStruct(tile.shape, jnp.bfloat16)] * 2,
        compiler_params=pltpu.CompilerParams(vmem_limit_bytes=24 * 2**20),
    )(tile)


def product_kernel(place, tile_high_ref, tile_low_ref, *refs):
    *block_refs, send_ref, keep_ref, high_ref, low_ref, held_high, held_low, arrived = refs
    height = block_refs[0].shape[0]
    half = send_ref.shape[0]

    def fetch(i, run):
        slot = i % 2
        run(pltpu.make_async_copy(tile_high_ref.at[place[1 + i]], held_high.at[slot], arrived.at[0, slot]))
        run(pltpu.make_async_copy(tile_low_ref.at[place[1 + i]], held_low.at[slot], arrived.at[1, slot]))

    fetch(0, lambda copy: copy.start())
    for j, block_ref in enumerate(block_refs):
        rows = pl.ds(pl.multiple_of((place[0] ^ j) * height, height), height)
        high_ref[rows], low_ref[rows] = parts(block_ref[...])

    def times(a, b_ref):
        return jnp.dot(a, b_ref[...], preferred_element_type=jnp.float32)

    for base, out_ref in ((0, send_ref), (half, keep_ref)):
        def step(i, carry):
            @pl.when(base + i + 1 < 2 * half)
            def _():
                fetch(base + i + 1, lambda copy: copy.start())

            fetch(base + i, lambda copy: copy.wait())
            high, low = held_high[(base + i) % 2], held_low[(base + i) % 2]
            out_ref[i] = times(high, high_ref) + (times(high, low_ref) + times(low, high_ref))
            return carry

        lax.fori_loop(0, half, step, 0)


def product(tiles, blocks):
    count, out_rows, width = tiles[0].shape
    columns = blocks[0].shape[1]
    half = count // 2
    chunks = lax.axis_index("col") ^ jnp.concatenate([2 * jnp.arange(half) + 1, 2 * jnp.arange(half)])
    place = jnp.concatenate([lax.axis_index("row")[None], chunks]).astype(jnp.int32)
    vmem, hbm = (pl.BlockSpec(memory_space=space) for space in (pltpu.VMEM, pltpu.HBM))
    return pl.pallas_call(
        product_kernel,
        in_specs=[pl.BlockSpec(memory_space=pltpu.SMEM), hbm, hbm] + [vmem] * len(blocks),
        out_specs=[vmem, vmem],
        out_shape=[jax.ShapeDtypeStruct((half, out_rows, columns), jnp.float32)] * 2,
        scratch_shapes=[pltpu.VMEM((width, columns), jnp.bfloat16)] * 2
        + [pltpu.VMEM((2, out_rows, width), jnp.bfloat16)] * 2
        + [pltpu.SemaphoreType.DMA((2, 2))],
        compiler_params=pltpu.CompilerParams(vmem_limit_bytes=24 * 2**20),
    )(place, *tiles, *blocks)


def dot(a, b, precision):
    return jnp.matmul(a, b, precision=precision)


def dot_tn(a, b, precision):
    return lax.dot_general(a, b, (((0,), (0,)), ((), ())), precision=precision)


def sum_scatter(blocks, axis, bit=1):
    while blocks.shape[0] > 1:
        pairs = blocks.reshape((blocks.shape[0] // 2, 2) + blocks.shape[1:])
        blocks = pairs[:, 0] + swap(pairs[:, 1], axis, bit)
        bit *= 2
    return blocks[0]


def sum_rows(blocks, axis):
    bit = 1
    while blocks.shape[0] > 1:
        mine = lax.axis_index(axis) // bit % 2
        pairs = blocks.reshape((blocks.shape[0] // 2, 2) + blocks.shape[1:])
        keep = lax.dynamic_index_in_dim(pairs, mine, 1, keepdims=False)
        blocks = keep + swap(lax.dynamic_index_in_dim(pairs, 1 - mine, 1, keepdims=False), axis, bit)
        bit *= 2
    return blocks[0]


def columns_by_xor(array, odd):
    cols, col_id = lax.axis_size("col"), lax.axis_index("col")
    span = array.shape[1] // cols
    return [lax.dynamic_slice_in_dim(array, (col_id ^ j) * span, span, 1) for j in range(odd, cols, 2)]


def source_col(row):
    return row * lax.axis_size("col") // lax.axis_size("row")


def blocks_to_send(blocks):
    rows, cols = lax.axis_size("row"), lax.axis_size("col")
    held = []
    for d in range(cols):
        wanted = [((r * cols + (source_col(r) ^ d)) % rows) ^ r for r in range(rows)]
        if len(set(wanted)) == 1:
            held.append(blocks[wanted[0]])
        else:
            held.append(lax.dynamic_index_in_dim(jnp.stack(blocks), jnp.array(wanted)[lax.axis_index("row")], 0, keepdims=False))
    return held


def spread_step(held):
    rows, cols = lax.axis_size("row"), lax.axis_size("col")
    bit = len(held) // 2
    pairs = [(r * cols + c, r * cols + (c ^ bit)) for r in range(rows) for c in range(cols)
             if (c ^ source_col(r)) % (2 * bit) == 0]
    moved = lax.ppermute(jnp.stack(held[bit:]), ("row", "col"), pairs)
    offset = lax.axis_index("col") ^ source_col(lax.axis_index("row"))
    return [jnp.where(offset & bit != 0, moved[j], held[j]) for j in range(bit)]


def local(inverse_tile, panels, link_panel, diag_inverse, ancestor_tiles):
    rows_axis, cols_axis = lax.axis_size("row"), lax.axis_size("col")
    row_id, col_id = lax.axis_index("row"), lax.axis_index("col")
    siblings, _, local_rows, width = panels.shape
    height, span = diag_inverse.shape[2:]
    row_start = (col_id * rows_axis + row_id) * local_rows
    tile_mask = jnp.repeat(ancestor_tiles, TILE, axis=2)
    kept_rows = lax.dynamic_slice_in_dim(tile_mask, row_start, local_rows, 2).astype(jnp.float32)
    masked = panels * kept_rows[..., None]
    tiles = [half.reshape(cols_axis, -1, half.shape[1]) for half in split(inverse_tile)]

    def one_pair(first, panel_second, link, given_first, given_second):
        live = {"tiles": tiles, "given": given_first, "first": first, "second": panel_second - dot(first, link, precise)}
        slots = {}

        def at(slot, *steps):
            slots.setdefault(slot, []).extend(steps)

        late = 2 * span
        pieces = [("first", i, i + late) for i in range(0, width, late)]
        count_first = len(pieces)
        pieces += [("second", i, i + late) for i in range(0, width, late)]
        stages = rows_axis.bit_length() - 1

        def fetch(k, stage):
            if stage == 0:
                panel, start, stop = pieces[k]
                live[k, 0] = live[panel][:, start:stop]
            for j in range(1, rows_axis):
                if j.bit_count() == stage + 1:
                    live[k, j] = swap(live[k, j & (j - 1)], "row", j & -j)

        def blocks(k):
            return [live[k, j] for j in range(rows_axis)]

        def multiply(k):
            if "tiles" in live:
                tiles[:] = live.pop("tiles")
            gathered = blocks(k)
            if ("sums", k - 1) in live:
                live["sums", k - 1], gathered = lax.optimization_barrier((live["sums", k - 1], gathered))
            live["send", k], live["keep", k] = product(tiles, gathered)

        def add_core(k):
            live["sums", k] = live.pop(("keep", k)) + swap(live.pop(("send", k)), "col", 1)

        def add_rest(k):
            live["out", k] = -sum_scatter(live.pop(("sums", k)), "col", 2)

        def collect(k):
            live["own", k] = blocks_to_send(blocks(k))
            spread(k)

        def spread(k):
            live["own", k] = spread_step(live["own", k])

        def owns(start, stop):
            return jnp.concatenate([live["own", k][0] for k in range(start, stop)], axis=1)

        def outs(start, stop):
            return jnp.concatenate([live["out", k] for k in range(start, stop)], axis=1)

        for k in range(len(pieces)):
            for stage in range(stages):
                at(k + stage, lambda k=k, stage=stage: fetch(k, stage))

        def link_terms():
            link_rows = lax.dynamic_slice_in_dim(link, row_id * height, height, 0)
            link_cols = lax.dynamic_slice_in_dim(link, col_id * span, span, 0)
            given = dot(live["given"], link_cols, precise)
            live["link_cross"] = lax.dynamic_update_slice_in_dim(jnp.zeros_like(link), given, row_id * height, 0)
            live["link_second"] = -dot_tn(link_rows, given, precise)

        def core_sum(terms):
            sent = swap(terms(1), "col", 1)
            return terms(0) + sent

        def spread_sum(sums):
            sums = sums.reshape(-1, cols_axis // 2, span).swapaxes(0, 1)
            sums = sum_scatter(sums, "col", 2)
            return sum_rows(sums.reshape(-1, rows_axis, height, span).swapaxes(0, 1), "row")

        def by_parity(array, odd):
            return jnp.concatenate(columns_by_xor(array, odd), axis=1)

        def first_terms():
            out_first = outs(0, count_first)
            own_first, own_second = owns(0, count_first), owns(count_first, len(pieces))

            def terms(odd):
                cross = dot_tn(out_first, by_parity(own_second, odd), three_pass) + by_parity(live["link_cross"], odd)
                return jnp.concatenate([dot_tn(out_first, by_parity(own_first, odd), three_pass), cross])

            live["first_sums"] = core_sum(terms)

        def first_sums():
            live["first_sums"] = spread_sum(live["first_sums"])

        def second_terms():
            out_second, own_second = outs(count_first, len(pieces)), owns(count_first, len(pieces))

            def terms(odd):
                return dot_tn(out_second, by_parity(own_second, odd), three_pass) + by_parity(live["link_second"], odd)

            live["second_sum"] = spread_sum(core_sum(terms))[0]

        at(1, link_terms)
        for k in range(len(pieces)):
            at(k + stages, lambda k=k: collect(k))
            for step in range(1, cols_axis.bit_length() - 1):
                at(k + stages + step, lambda k=k: spread(k))
        for k in range(len(pieces)):
            at(k + stages + 1, lambda k=k: add_core(k))
            at(k + stages, lambda k=k: multiply(k))
        for k in range(len(pieces)):
            at(k + stages + 1, lambda k=k: add_rest(k))
        end = len(pieces) + stages + 1
        at(end - 1, first_terms)
        at(end, first_sums, second_terms)

        for slot in range(end + 1):
            if slot > 0:
                live = dict(zip(live, lax.optimization_barrier(list(live.values()))))
            for step in slots[slot]:
                step()

        first_sum, cross_sum = live["first_sums"]
        ancestor = jnp.stack([outs(0, count_first), outs(count_first, len(pieces))])
        diagonal = jnp.stack([given_first - first_sum, given_second - live["second_sum"]])
        return ancestor, diagonal, -cross_sum

    results = [one_pair(masked[s, 0], masked[s, 1], link_panel[s], diag_inverse[s, 0], diag_inverse[s, 1])
               for s in range(siblings)]
    return tuple(jnp.stack(group) for group in zip(*results))


def solution(mesh):
    in_specs = (
        P(("hyp", "row"), "col"),
        P("hyp", None, ("col", "row"), None),
        P("hyp", None, None),
        P("hyp", None, "row", "col"),
        P(),
    )
    out_specs = (
        P("hyp", None, ("row", "col"), None),
        P("hyp", None, "row", "col"),
        P("hyp", "row", "col"),
    )
    return jax.shard_map(local, mesh=mesh, in_specs=in_specs, out_specs=out_specs, check_vma=False)
```

```python
import jax
import jax.numpy as jnp
from jax import lax
from jax.experimental import pallas as pl
from jax.experimental.pallas import tpu as pltpu
from jax.sharding import PartitionSpec as P

TILE = 128

precise = lax.Precision.HIGHEST
three_pass = lax.Precision.HIGH


def swap(block, axis, bit):
    pairs = [(i, i ^ bit) for i in range(lax.axis_size(axis))]
    return lax.ppermute(block, axis, pairs)


def parts(values):
    high = values.astype(jnp.bfloat16)
    return high, (values - high.astype(jnp.float32)).astype(jnp.bfloat16)


PARTS = 6


def split_kernel(tile_ref, parts_ref):
    parts_ref[0], parts_ref[1] = parts(tile_ref[...])


def split(tile):
    rows, width = tile.shape
    step = min(rows, 256)
    return pl.pallas_call(
        split_kernel,
        grid=(rows // step,),
        in_specs=[pl.BlockSpec((step, width), lambda t: (t, 0))],
        out_specs=pl.BlockSpec((2, step, width), lambda t: (0, t, 0)),
        out_shape=jax.ShapeDtypeStruct((PARTS, rows, width), jnp.bfloat16),
        compiler_params=pltpu.CompilerParams(vmem_limit_bytes=24 * 2**20),
    )(tile)


def product_kernel(place, tile_ref, *refs):
    *block_refs, send_ref, keep_ref, high_ref, low_ref, held, arrived = refs
    height = block_refs[0].shape[0]
    half = send_ref.shape[0]

    def fetch(i, run):
        slot = i % 2
        for part in range(2):
            run(pltpu.make_async_copy(tile_ref.at[part, place[1 + i]], held.at[part, slot], arrived.at[part, slot]))

    fetch(0, lambda copy: copy.start())
    for j, block_ref in enumerate(block_refs):
        rows = pl.ds(pl.multiple_of((place[0] ^ j) * height, height), height)
        high_ref[rows], low_ref[rows] = parts(block_ref[...])

    def times(a, b_ref):
        return jnp.dot(a, b_ref[...], preferred_element_type=jnp.float32)

    for base, out_ref in ((0, send_ref), (half, keep_ref)):
        def step(i, carry):
            @pl.when(base + i + 1 < 2 * half)
            def _():
                fetch(base + i + 1, lambda copy: copy.start())

            fetch(base + i, lambda copy: copy.wait())
            high, low = held[0, (base + i) % 2], held[1, (base + i) % 2]
            out_ref[i] = times(high, high_ref) + (times(high, low_ref) + times(low, high_ref))
            return carry

        lax.fori_loop(0, half, step, 0)


def product(tile, blocks):
    _, count, out_rows, width = tile.shape
    columns = blocks[0].shape[1]
    half = count // 2
    chunks = lax.axis_index("col") ^ jnp.concatenate([2 * jnp.arange(half) + 1, 2 * jnp.arange(half)])
    place = jnp.concatenate([lax.axis_index("row")[None], chunks]).astype(jnp.int32)
    vmem, hbm = (pl.BlockSpec(memory_space=space) for space in (pltpu.VMEM, pltpu.HBM))
    return pl.pallas_call(
        product_kernel,
        in_specs=[pl.BlockSpec(memory_space=pltpu.SMEM), hbm] + [vmem] * len(blocks),
        out_specs=[vmem, vmem],
        out_shape=[jax.ShapeDtypeStruct((half, out_rows, columns), jnp.float32)] * 2,
        scratch_shapes=[pltpu.VMEM((width, columns), jnp.bfloat16)] * 2
        + [pltpu.VMEM((2, 2, out_rows, width), jnp.bfloat16), pltpu.SemaphoreType.DMA((2, 2))],
        compiler_params=pltpu.CompilerParams(vmem_limit_bytes=24 * 2**20),
    )(place, tile, *blocks)


def dot(a, b, precision):
    return jnp.matmul(a, b, precision=precision)


def dot_tn(a, b, precision):
    return lax.dot_general(a, b, (((0,), (0,)), ((), ())), precision=precision)


def sum_scatter(blocks, axis, bit=1):
    while blocks.shape[0] > 1:
        pairs = blocks.reshape((blocks.shape[0] // 2, 2) + blocks.shape[1:])
        blocks = pairs[:, 0] + swap(pairs[:, 1], axis, bit)
        bit *= 2
    return blocks[0]


def sum_step(blocks, axis, bit):
    mine = lax.axis_index(axis) // bit % 2
    pairs = blocks.reshape((blocks.shape[0] // 2, 2) + blocks.shape[1:])
    keep = lax.dynamic_index_in_dim(pairs, mine, 1, keepdims=False)
    return keep + swap(lax.dynamic_index_in_dim(pairs, 1 - mine, 1, keepdims=False), axis, bit)


def sum_rows(blocks, axis, bit=1):
    while blocks.shape[0] > 1:
        blocks = sum_step(blocks, axis, bit)
        bit *= 2
    return blocks[0]


def columns_by_xor(array, odd):
    cols, col_id = lax.axis_size("col"), lax.axis_index("col")
    span = array.shape[1] // cols
    return [lax.dynamic_slice_in_dim(array, (col_id ^ j) * span, span, 1) for j in range(odd, cols, 2)]


def source_col(row):
    return row * lax.axis_size("col") // lax.axis_size("row")


def blocks_to_send(blocks):
    rows, cols = lax.axis_size("row"), lax.axis_size("col")
    held = []
    for d in range(cols):
        wanted = [((r * cols + (source_col(r) ^ d)) % rows) ^ r for r in range(rows)]
        if len(set(wanted)) == 1:
            held.append(blocks[wanted[0]])
        else:
            held.append(lax.dynamic_index_in_dim(jnp.stack(blocks), jnp.array(wanted)[lax.axis_index("row")], 0, keepdims=False))
    return held


def spread_step(held):
    rows, cols = lax.axis_size("row"), lax.axis_size("col")
    bit = len(held) // 2
    pairs = [(r * cols + c, r * cols + (c ^ bit)) for r in range(rows) for c in range(cols)
             if (c ^ source_col(r)) % (2 * bit) == 0]
    moved = lax.ppermute(jnp.stack(held[bit:]), ("row", "col"), pairs)
    offset = lax.axis_index("col") ^ source_col(lax.axis_index("row"))
    return [jnp.where(offset & bit != 0, moved[j], held[j]) for j in range(bit)]


def local(inverse_tile, panels, link_panel, diag_inverse, ancestor_tiles):
    rows_axis, cols_axis = lax.axis_size("row"), lax.axis_size("col")
    row_id, col_id = lax.axis_index("row"), lax.axis_index("col")
    siblings, _, local_rows, width = panels.shape
    height, span = diag_inverse.shape[2:]
    row_start = (col_id * rows_axis + row_id) * local_rows
    tile_mask = jnp.repeat(ancestor_tiles, TILE, axis=2)
    kept_rows = lax.dynamic_slice_in_dim(tile_mask, row_start, local_rows, 2).astype(jnp.float32)
    masked = panels * kept_rows[..., None]
    tile = split(inverse_tile).reshape(PARTS, cols_axis, -1, inverse_tile.shape[1])

    def one_pair(first, panel_second, link, given_first, given_second):
        live = {"tile": tile, "given": given_first, "first": first, "second": panel_second - dot(first, link, precise)}
        slots = {}

        def at(slot, *steps):
            slots.setdefault(slot, []).extend(steps)

        late = 2 * span
        pieces = [("first", i, i + late) for i in range(0, width, late)]
        count_first = len(pieces)
        pieces += [("second", i, i + late) for i in range(0, width, late)]
        stages = rows_axis.bit_length() - 1

        def fetch(k, stage):
            if stage == 0:
                panel, start, stop = pieces[k]
                live[k, 0] = live[panel][:, start:stop]
            for j in range(1, rows_axis):
                if j.bit_count() == stage + 1:
                    live[k, j] = swap(live[k, j & (j - 1)], "row", j & -j)

        def blocks(k):
            return [live[k, j] for j in range(rows_axis)]

        def multiply(k):
            gathered = blocks(k)
            if ("sums", k - 1) in live:
                live["sums", k - 1], gathered = lax.optimization_barrier((live["sums", k - 1], gathered))
            live["send", k], live["keep", k] = product(live["tile"], gathered)

        def add_core(k):
            live["sums", k] = live.pop(("keep", k)) + swap(live.pop(("send", k)), "col", 1)

        def add_rest(k):
            live["out", k] = -sum_scatter(live.pop(("sums", k)), "col", 2)

        def collect(k):
            live["own", k] = blocks_to_send(blocks(k))
            spread(k)

        def spread(k):
            live["own", k] = spread_step(live["own", k])

        def owns(start, stop):
            return jnp.concatenate([live["own", k][0] for k in range(start, stop)], axis=1)

        def outs(start, stop):
            return jnp.concatenate([live["out", k] for k in range(start, stop)], axis=1)

        for k in range(len(pieces)):
            for stage in range(stages):
                at(k + stage, lambda k=k, stage=stage: fetch(k, stage))

        def link_terms():
            link_rows = lax.dynamic_slice_in_dim(link, row_id * height, height, 0)
            link_cols = lax.dynamic_slice_in_dim(link, col_id * span, span, 0)
            given = dot(live["given"], link_cols, precise)
            live["link_cross"] = lax.dynamic_update_slice_in_dim(jnp.zeros_like(link), given, row_id * height, 0)
            live["link_second"] = -dot_tn(link_rows, given, precise)

        def core_sum(terms):
            sent = swap(terms(1), "col", 1)
            return terms(0) + sent

        def by_rows(sums):
            return sums.reshape(-1, rows_axis, height, sums.shape[1]).swapaxes(0, 1)

        def rest_of_cols(sums):
            return sum_scatter(sums.reshape(-1, cols_axis // 2, span).swapaxes(0, 1), "col", 2)

        def by_parity(array, odd):
            return jnp.concatenate(columns_by_xor(array, odd), axis=1)

        def first_terms():
            out_first = outs(0, count_first)
            own_first, own_second = owns(0, count_first), owns(count_first, len(pieces))

            def terms(odd):
                cross = dot_tn(out_first, by_parity(own_second, odd), three_pass) + by_parity(live["link_cross"], odd)
                return jnp.concatenate([dot_tn(out_first, by_parity(own_first, odd), three_pass), cross])

            live["first_sums"] = sum_step(by_rows(core_sum(terms)), "row", 1)

        def first_sums():
            sums = sum_rows(live["first_sums"], "row", 2)
            live["first_sums"] = rest_of_cols(sums.reshape(-1, sums.shape[2])).reshape(-1, height, span)

        def second_terms():
            out_second, own_second = outs(count_first, len(pieces)), owns(count_first, len(pieces))

            def terms(odd):
                return dot_tn(out_second, by_parity(own_second, odd), three_pass) + by_parity(live["link_second"], odd)

            live["second_sum"] = sum_rows(by_rows(rest_of_cols(core_sum(terms))), "row")[0]

        at(1, link_terms)
        for k in range(len(pieces)):
            at(k + stages, lambda k=k: collect(k))
            for step in range(1, cols_axis.bit_length() - 1):
                at(k + stages + step, lambda k=k: spread(k))
        for k in range(len(pieces)):
            at(k + stages + 1, lambda k=k: add_core(k))
            at(k + stages, lambda k=k: multiply(k))
        for k in range(len(pieces)):
            at(k + stages + 1, lambda k=k: add_rest(k))
        end = len(pieces) + stages + 1
        at(end - 1, first_terms)
        at(end, first_sums, second_terms)

        for slot in range(end + 1):
            if slot > 0:
                live = dict(zip(live, lax.optimization_barrier(list(live.values()))))
            for step in slots[slot]:
                step()

        first_sum, cross_sum = live["first_sums"]
        ancestor = jnp.stack([outs(0, count_first), outs(count_first, len(pieces))])
        diagonal = jnp.stack([given_first - first_sum, given_second - live["second_sum"]])
        return ancestor, diagonal, -cross_sum

    results = [one_pair(masked[s, 0], masked[s, 1], link_panel[s], diag_inverse[s, 0], diag_inverse[s, 1])
               for s in range(siblings)]
    return tuple(jnp.stack(group) for group in zip(*results))


def solution(mesh):
    in_specs = (
        P(("hyp", "row"), "col"),
        P("hyp", None, ("col", "row"), None),
        P("hyp", None, None),
        P("hyp", None, "row", "col"),
        P(),
    )
    out_specs = (
        P("hyp", None, ("row", "col"), None),
        P("hyp", None, "row", "col"),
        P("hyp", "row", "col"),
    )
    return jax.shard_map(local, mesh=mesh, in_specs=in_specs, out_specs=out_specs, check_vma=False)
```

```python
import jax
import jax.numpy as jnp
from jax import lax
from jax.experimental import pallas as pl
from jax.experimental.pallas import tpu as pltpu
from jax.sharding import PartitionSpec as P

TILE = 128

precise = lax.Precision.HIGHEST
three_pass = lax.Precision.HIGH


def swap(block, axis, bit):
    pairs = [(i, i ^ bit) for i in range(lax.axis_size(axis))]
    return lax.ppermute(block, axis, pairs)


def parts(values):
    high = values.astype(jnp.bfloat16)
    return high, (values - high.astype(jnp.float32)).astype(jnp.bfloat16)


PARTS = 6


def split_kernel(tile_ref, parts_ref):
    parts_ref[0], parts_ref[1] = parts(tile_ref[...])


def split(tile):
    rows, width = tile.shape
    step = min(rows, 256)
    return pl.pallas_call(
        split_kernel,
        grid=(rows // step,),
        in_specs=[pl.BlockSpec((step, width), lambda t: (t, 0))],
        out_specs=pl.BlockSpec((2, step, width), lambda t: (0, t, 0)),
        out_shape=jax.ShapeDtypeStruct((PARTS, rows, width), jnp.bfloat16),
        compiler_params=pltpu.CompilerParams(vmem_limit_bytes=24 * 2**20),
    )(tile)


def product_kernel(place, tile_ref, *refs):
    *block_refs, send_ref, keep_ref, high_ref, low_ref, held, arrived = refs
    height = block_refs[0].shape[0]
    half = send_ref.shape[0]

    def fetch(i, run):
        slot = i % 2
        for part in range(2):
            run(pltpu.make_async_copy(tile_ref.at[part, place[1 + i]], held.at[part, slot], arrived.at[part, slot]))

    fetch(0, lambda copy: copy.start())
    for j, block_ref in enumerate(block_refs):
        rows = pl.ds(pl.multiple_of((place[0] ^ j) * height, height), height)
        high_ref[rows], low_ref[rows] = parts(block_ref[...])

    def times(a, b_ref):
        return jnp.dot(a, b_ref[...], preferred_element_type=jnp.float32)

    for base, out_ref in ((0, send_ref), (half, keep_ref)):
        def step(i, carry):
            @pl.when(base + i + 1 < 2 * half)
            def _():
                fetch(base + i + 1, lambda copy: copy.start())

            fetch(base + i, lambda copy: copy.wait())
            high, low = held[0, (base + i) % 2], held[1, (base + i) % 2]
            out_ref[i] = times(high, high_ref) + (times(high, low_ref) + times(low, high_ref))
            return carry

        lax.fori_loop(0, half, step, 0)


def product(tile, blocks):
    _, count, out_rows, width = tile.shape
    columns = blocks[0].shape[1]
    half = count // 2
    chunks = lax.axis_index("col") ^ jnp.concatenate([2 * jnp.arange(half) + 1, 2 * jnp.arange(half)])
    place = jnp.concatenate([lax.axis_index("row")[None], chunks]).astype(jnp.int32)
    vmem, hbm = (pl.BlockSpec(memory_space=space) for space in (pltpu.VMEM, pltpu.HBM))
    return pl.pallas_call(
        product_kernel,
        in_specs=[pl.BlockSpec(memory_space=pltpu.SMEM), hbm] + [vmem] * len(blocks),
        out_specs=[vmem, vmem],
        out_shape=[jax.ShapeDtypeStruct((half, out_rows, columns), jnp.float32)] * 2,
        scratch_shapes=[pltpu.VMEM((width, columns), jnp.bfloat16)] * 2
        + [pltpu.VMEM((2, 2, out_rows, width), jnp.bfloat16), pltpu.SemaphoreType.DMA((2, 2))],
        compiler_params=pltpu.CompilerParams(vmem_limit_bytes=24 * 2**20),
    )(place, tile, *blocks)


def dot(a, b, precision):
    return jnp.matmul(a, b, precision=precision)


def dot_tn(a, b, precision):
    return lax.dot_general(a, b, (((0,), (0,)), ((), ())), precision=precision)


def sum_scatter(blocks, axis, bit=1):
    while blocks.shape[0] > 1:
        pairs = blocks.reshape((blocks.shape[0] // 2, 2) + blocks.shape[1:])
        blocks = pairs[:, 0] + swap(pairs[:, 1], axis, bit)
        bit *= 2
    return blocks[0]


def sum_step(blocks, axis, bit):
    mine = lax.axis_index(axis) // bit % 2
    pairs = blocks.reshape((blocks.shape[0] // 2, 2) + blocks.shape[1:])
    keep = lax.dynamic_index_in_dim(pairs, mine, 1, keepdims=False)
    return keep + swap(lax.dynamic_index_in_dim(pairs, 1 - mine, 1, keepdims=False), axis, bit)


def sum_rows(blocks, axis, bit=1):
    while blocks.shape[0] > 1:
        blocks = sum_step(blocks, axis, bit)
        bit *= 2
    return blocks[0]


def columns_by_xor(array, odd):
    cols, col_id = lax.axis_size("col"), lax.axis_index("col")
    span = array.shape[1] // cols
    return [lax.dynamic_slice_in_dim(array, (col_id ^ j) * span, span, 1) for j in range(odd, cols, 2)]


def source_col(row):
    return row * lax.axis_size("col") // lax.axis_size("row")


def blocks_to_send(blocks):
    rows, cols = lax.axis_size("row"), lax.axis_size("col")
    held = []
    for d in range(cols):
        wanted = [((r * cols + (source_col(r) ^ d)) % rows) ^ r for r in range(rows)]
        if len(set(wanted)) == 1:
            held.append(blocks[wanted[0]])
        else:
            held.append(lax.dynamic_index_in_dim(jnp.stack(blocks), jnp.array(wanted)[lax.axis_index("row")], 0, keepdims=False))
    return held


def spread_step(held):
    rows, cols = lax.axis_size("row"), lax.axis_size("col")
    bit = len(held) // 2
    pairs = [(r * cols + c, r * cols + (c ^ bit)) for r in range(rows) for c in range(cols)
             if (c ^ source_col(r)) % (2 * bit) == 0]
    moved = lax.ppermute(jnp.stack(held[bit:]), ("row", "col"), pairs)
    offset = lax.axis_index("col") ^ source_col(lax.axis_index("row"))
    return [jnp.where(offset & bit != 0, moved[j], held[j]) for j in range(bit)]


def local(inverse_tile, panels, link_panel, diag_inverse, ancestor_tiles):
    rows_axis, cols_axis = lax.axis_size("row"), lax.axis_size("col")
    row_id, col_id = lax.axis_index("row"), lax.axis_index("col")
    siblings, _, local_rows, width = panels.shape
    height, span = diag_inverse.shape[2:]
    row_start = (col_id * rows_axis + row_id) * local_rows
    tile_mask = jnp.repeat(ancestor_tiles, TILE, axis=2)
    kept_rows = lax.dynamic_slice_in_dim(tile_mask, row_start, local_rows, 2).astype(jnp.float32)
    tile = split(inverse_tile).reshape(PARTS, cols_axis, -1, inverse_tile.shape[1])

    def one_pair(panels, kept_first, kept_second, link, given_first, given_second):
        live = {"tile": tile, "given": given_first}
        slots = {}

        def at(slot, *steps):
            slots.setdefault(slot, []).extend(steps)

        late = 2 * span
        pieces = [("first", i, i + late) for i in range(0, width, late)]
        count_first = len(pieces)
        pieces += [("second", i, i + late) for i in range(0, width, late)]
        stages = rows_axis.bit_length() - 1
        second = panels[1] * kept_second - dot(panels[0] * kept_first, link, precise)
        for k, (panel, start, stop) in enumerate(pieces):
            live["piece", k] = panels[0][:, start:stop] * kept_first if panel == "first" else second[:, start:stop]

        def fetch(k, stage):
            if stage == 0:
                live[k, 0] = live.pop(("piece", k))
            for j in reversed(range(1, rows_axis)):
                if j.bit_count() == stage + 1:
                    live[k, j] = swap(live[k, j & (j - 1)], "row", j & -j)

        def blocks(k):
            return [live[k, j] for j in range(rows_axis)]

        def multiply(k):
            gathered = blocks(k)
            if ("sums", k - 1) in live:
                live["sums", k - 1], gathered = lax.optimization_barrier((live["sums", k - 1], gathered))
            live["send", k], live["keep", k] = product(live["tile"], gathered)

        def add_core(k):
            live["sums", k] = live.pop(("keep", k)) + swap(live.pop(("send", k)), "col", 1)

        def add_rest(k):
            live["out", k] = -sum_scatter(live.pop(("sums", k)), "col", 2)

        def collect(k):
            live["own", k] = blocks_to_send(blocks(k))
            spread(k)

        def spread(k):
            live["own", k] = spread_step(live["own", k])

        def owns(start, stop):
            return jnp.concatenate([live["own", k][0] for k in range(start, stop)], axis=1)

        def outs(start, stop):
            return jnp.concatenate([live["out", k] for k in range(start, stop)], axis=1)

        for k in range(len(pieces)):
            for stage in range(stages):
                at(k + stage, lambda k=k, stage=stage: fetch(k, stage))

        def link_terms():
            link_rows = lax.dynamic_slice_in_dim(link, row_id * height, height, 0)
            link_cols = lax.dynamic_slice_in_dim(link, col_id * span, span, 0)
            given = dot(live["given"], link_cols, precise)
            live["link_cross"] = lax.dynamic_update_slice_in_dim(jnp.zeros_like(link), given, row_id * height, 0)
            live["link_second"] = -dot_tn(link_rows, given, precise)

        def core_sum(terms):
            sent = swap(terms(1), "col", 1)
            return terms(0) + sent

        def by_rows(sums):
            return sums.reshape(-1, rows_axis, height, sums.shape[1]).swapaxes(0, 1)

        def rest_of_cols(sums):
            return sum_scatter(sums.reshape(-1, cols_axis // 2, span).swapaxes(0, 1), "col", 2)

        def by_parity(array, odd):
            return jnp.concatenate(columns_by_xor(array, odd), axis=1)

        def first_terms():
            out_first = outs(0, count_first)
            own_first, own_second = owns(0, count_first), owns(count_first, len(pieces))

            def terms(odd):
                cross = dot_tn(out_first, by_parity(own_second, odd), three_pass) + by_parity(live["link_cross"], odd)
                return jnp.concatenate([dot_tn(out_first, by_parity(own_first, odd), three_pass), cross])

            live["first_sums"] = sum_step(by_rows(core_sum(terms)), "row", 1)

        def first_sums():
            sums = sum_rows(live["first_sums"], "row", 2)
            live["first_sums"] = rest_of_cols(sums.reshape(-1, sums.shape[2])).reshape(-1, height, span)

        def second_terms():
            out_second, own_second = outs(count_first, len(pieces)), owns(count_first, len(pieces))

            def terms(odd):
                return dot_tn(out_second, by_parity(own_second, odd), three_pass) + by_parity(live["link_second"], odd)

            live["second_sum"] = sum_rows(by_rows(rest_of_cols(core_sum(terms))), "row")[0]

        at(1, link_terms)
        last = len(pieces) - 1 + stages
        for k in range(len(pieces)):
            at(k + stages, lambda k=k: collect(k))
            for step in range(1, cols_axis.bit_length() - 1):
                at(k + stages + step, lambda k=k: spread(k))
        for k in range(len(pieces)):
            at(k + stages + 1, lambda k=k: add_core(k))
            at(k + stages, lambda k=k: multiply(k))
        for k in range(len(pieces)):
            at(k + stages + 1, lambda k=k: add_rest(k))
        end = last + 2
        at(last + 1, first_terms)
        at(end, first_sums, second_terms)

        for slot in range(end + 1):
            if slot > 0:
                live = dict(zip(live, lax.optimization_barrier(list(live.values()))))
            for step in slots[slot]:
                step()

        first_sum, cross_sum = live["first_sums"]
        ancestor = jnp.stack([outs(0, count_first), outs(count_first, len(pieces))])
        diagonal = jnp.stack([given_first - first_sum, given_second - live["second_sum"]])
        return ancestor, diagonal, -cross_sum

    results = [one_pair(panels[s], kept_rows[s, 0, :, None], kept_rows[s, 1, :, None], link_panel[s],
                        diag_inverse[s, 0], diag_inverse[s, 1])
               for s in range(siblings)]
    return tuple(jnp.stack(group) for group in zip(*results))


def solution(mesh):
    in_specs = (
        P(("hyp", "row"), "col"),
        P("hyp", None, ("col", "row"), None),
        P("hyp", None, None),
        P("hyp", None, "row", "col"),
        P(),
    )
    out_specs = (
        P("hyp", None, ("row", "col"), None),
        P("hyp", None, "row", "col"),
        P("hyp", "row", "col"),
    )
    return jax.shard_map(local, mesh=mesh, in_specs=in_specs, out_specs=out_specs, check_vma=False)
```

```python
import jax
import jax.numpy as jnp
from jax import lax
from jax.experimental import pallas as pl
from jax.experimental.pallas import tpu as pltpu
from jax.sharding import PartitionSpec as P

TILE = 128

precise = lax.Precision.HIGHEST
three_pass = lax.Precision.HIGH


def swap(block, axis, bit):
    pairs = [(i, i ^ bit) for i in range(lax.axis_size(axis))]
    return lax.ppermute(block, axis, pairs)


def parts(values):
    high = values.astype(jnp.bfloat16)
    return high, (values - high.astype(jnp.float32)).astype(jnp.bfloat16)


PARTS = 6


def split_kernel(tile_ref, parts_ref):
    parts_ref[0], parts_ref[1] = parts(tile_ref[...])


def split(tile):
    rows, width = tile.shape
    step = min(rows, 256)
    return pl.pallas_call(
        split_kernel,
        grid=(rows // step,),
        in_specs=[pl.BlockSpec((step, width), lambda t: (t, 0))],
        out_specs=pl.BlockSpec((2, step, width), lambda t: (0, t, 0)),
        out_shape=jax.ShapeDtypeStruct((PARTS, rows, width), jnp.bfloat16),
        compiler_params=pltpu.CompilerParams(vmem_limit_bytes=24 * 2**20),
    )(tile)


def product_kernel(place, tile_ref, *refs):
    *block_refs, send_ref, keep_ref, high_ref, low_ref, held, arrived = refs
    height = block_refs[0].shape[0]
    half = send_ref.shape[0]

    def fetch(i, run):
        slot = i % 2
        for part in range(2):
            run(pltpu.make_async_copy(tile_ref.at[part, place[1 + i]], held.at[part, slot], arrived.at[part, slot]))

    fetch(0, lambda copy: copy.start())
    for j, block_ref in enumerate(block_refs):
        rows = pl.ds(pl.multiple_of((place[0] ^ j) * height, height), height)
        high_ref[rows], low_ref[rows] = parts(block_ref[...])

    def times(a, b_ref):
        return jnp.dot(a, b_ref[...], preferred_element_type=jnp.float32)

    for base, out_ref in ((0, send_ref), (half, keep_ref)):
        def step(i, carry):
            @pl.when(base + i + 1 < 2 * half)
            def _():
                fetch(base + i + 1, lambda copy: copy.start())

            fetch(base + i, lambda copy: copy.wait())
            high, low = held[0, (base + i) % 2], held[1, (base + i) % 2]
            out_ref[i] = times(high, high_ref) + (times(high, low_ref) + times(low, high_ref))
            return carry

        lax.fori_loop(0, half, step, 0)


def product(tile, blocks):
    _, count, out_rows, width = tile.shape
    columns = blocks[0].shape[1]
    half = count // 2
    chunks = lax.axis_index("col") ^ jnp.concatenate([2 * jnp.arange(half) + 1, 2 * jnp.arange(half)])
    place = jnp.concatenate([lax.axis_index("row")[None], chunks]).astype(jnp.int32)
    vmem, hbm = (pl.BlockSpec(memory_space=space) for space in (pltpu.VMEM, pltpu.HBM))
    return pl.pallas_call(
        product_kernel,
        in_specs=[pl.BlockSpec(memory_space=pltpu.SMEM), hbm] + [vmem] * len(blocks),
        out_specs=[vmem, vmem],
        out_shape=[jax.ShapeDtypeStruct((half, out_rows, columns), jnp.float32)] * 2,
        scratch_shapes=[pltpu.VMEM((width, columns), jnp.bfloat16)] * 2
        + [pltpu.VMEM((2, 2, out_rows, width), jnp.bfloat16), pltpu.SemaphoreType.DMA((2, 2))],
        compiler_params=pltpu.CompilerParams(vmem_limit_bytes=24 * 2**20),
    )(place, tile, *blocks)


def dot(a, b, precision):
    return jnp.matmul(a, b, precision=precision)


def dot_tn(a, b, precision):
    return lax.dot_general(a, b, (((0,), (0,)), ((), ())), precision=precision)


def sum_scatter(blocks, axis, bit=1):
    while blocks.shape[0] > 1:
        pairs = blocks.reshape((blocks.shape[0] // 2, 2) + blocks.shape[1:])
        blocks = pairs[:, 0] + swap(pairs[:, 1], axis, bit)
        bit *= 2
    return blocks[0]


def sum_step(blocks, axis, bit):
    mine = lax.axis_index(axis) // bit % 2
    pairs = blocks.reshape((blocks.shape[0] // 2, 2) + blocks.shape[1:])
    keep = lax.dynamic_index_in_dim(pairs, mine, 1, keepdims=False)
    return keep + swap(lax.dynamic_index_in_dim(pairs, 1 - mine, 1, keepdims=False), axis, bit)


def sum_rows(blocks, axis, bit=1):
    while blocks.shape[0] > 1:
        blocks = sum_step(blocks, axis, bit)
        bit *= 2
    return blocks[0]


def columns_by_xor(array, odd):
    cols, col_id = lax.axis_size("col"), lax.axis_index("col")
    span = array.shape[1] // cols
    return [lax.dynamic_slice_in_dim(array, (col_id ^ j) * span, span, 1) for j in range(odd, cols, 2)]


def source_col(row):
    return row * lax.axis_size("col") // lax.axis_size("row")


def blocks_to_send(blocks):
    rows, cols = lax.axis_size("row"), lax.axis_size("col")
    held = []
    for d in range(cols):
        wanted = [((r * cols + (source_col(r) ^ d)) % rows) ^ r for r in range(rows)]
        if len(set(wanted)) == 1:
            held.append(blocks[wanted[0]])
        else:
            held.append(lax.dynamic_index_in_dim(jnp.stack(blocks), jnp.array(wanted)[lax.axis_index("row")], 0, keepdims=False))
    return held


def spread_step(held):
    rows, cols = lax.axis_size("row"), lax.axis_size("col")
    bit = len(held) // 2
    pairs = [(r * cols + c, r * cols + (c ^ bit)) for r in range(rows) for c in range(cols)
             if (c ^ source_col(r)) % (2 * bit) == 0]
    moved = lax.ppermute(jnp.stack(held[bit:]), ("row", "col"), pairs)
    offset = lax.axis_index("col") ^ source_col(lax.axis_index("row"))
    return [jnp.where(offset & bit != 0, moved[j], held[j]) for j in range(bit)]


def local(inverse_tile, panels, link_panel, diag_inverse, ancestor_tiles):
    rows_axis, cols_axis = lax.axis_size("row"), lax.axis_size("col")
    row_id, col_id = lax.axis_index("row"), lax.axis_index("col")
    siblings, _, local_rows, width = panels.shape
    height, span = diag_inverse.shape[2:]
    row_start = (col_id * rows_axis + row_id) * local_rows
    tile_mask = jnp.repeat(ancestor_tiles, TILE, axis=2)
    kept_rows = lax.dynamic_slice_in_dim(tile_mask, row_start, local_rows, 2).astype(jnp.float32)
    tile = split(inverse_tile).reshape(PARTS, cols_axis, -1, inverse_tile.shape[1])

    def one_pair(panels, kept_first, kept_second, link, given_first, given_second):
        live = {"tile": tile, "given": given_first}
        slots = {}

        def at(slot, *steps):
            slots.setdefault(slot, []).extend(steps)

        late = 2 * span
        pieces = [("first", i, i + late) for i in range(0, width, late)]
        count_first = len(pieces)
        pieces += [("second", i, i + late) for i in range(0, width - late, late)]
        pieces += [("second", i, i + span) for i in range(width - late, width, span)]
        stages = rows_axis.bit_length() - 1
        second = panels[1] * kept_second - dot(panels[0] * kept_first, link, precise)
        for k, (panel, start, stop) in enumerate(pieces):
            live["piece", k] = panels[0][:, start:stop] * kept_first if panel == "first" else second[:, start:stop]

        def fetch(k, stage):
            if stage == 0:
                live[k, 0] = live.pop(("piece", k))
            for j in reversed(range(1, rows_axis)):
                if j.bit_count() == stage + 1:
                    live[k, j] = swap(live[k, j & (j - 1)], "row", j & -j)

        def blocks(k):
            return [live[k, j] for j in range(rows_axis)]

        def multiply(k):
            gathered = blocks(k)
            if ("sums", k - 1) in live:
                live["sums", k - 1], gathered = lax.optimization_barrier((live["sums", k - 1], gathered))
            live["send", k], live["keep", k] = product(live["tile"], gathered)

        def add_core(k):
            live["sums", k] = live.pop(("keep", k)) + swap(live.pop(("send", k)), "col", 1)

        def add_rest(k):
            live["out", k] = -sum_scatter(live.pop(("sums", k)), "col", 2)

        def collect(k):
            live["own", k] = blocks_to_send(blocks(k))
            spread(k)

        def spread(k):
            live["own", k] = spread_step(live["own", k])

        def owns(start, stop):
            return jnp.concatenate([live["own", k][0] for k in range(start, stop)], axis=1)

        def outs(start, stop):
            return jnp.concatenate([live["out", k] for k in range(start, stop)], axis=1)

        for k in range(len(pieces)):
            for stage in range(stages):
                at(k + stage, lambda k=k, stage=stage: fetch(k, stage))

        def link_terms():
            link_rows = lax.dynamic_slice_in_dim(link, row_id * height, height, 0)
            link_cols = lax.dynamic_slice_in_dim(link, col_id * span, span, 0)
            given = dot(live["given"], link_cols, precise)
            live["link_cross"] = lax.dynamic_update_slice_in_dim(jnp.zeros_like(link), given, row_id * height, 0)
            live["link_second"] = -dot_tn(link_rows, given, precise)

        def core_sum(terms):
            sent = swap(terms(1), "col", 1)
            return terms(0) + sent

        def by_rows(sums):
            return sums.reshape(-1, rows_axis, height, sums.shape[1]).swapaxes(0, 1)

        def rest_of_cols(sums):
            return sum_scatter(sums.reshape(-1, cols_axis // 2, span).swapaxes(0, 1), "col", 2)

        def by_parity(array, odd):
            return jnp.concatenate(columns_by_xor(array, odd), axis=1)

        def first_terms():
            out_first, own_first = outs(0, count_first), owns(0, count_first)
            sums = core_sum(lambda odd: dot_tn(out_first, by_parity(own_first, odd), three_pass))
            live["first_sum"] = by_rows(rest_of_cols(sums))

        def first_rows():
            live["first_sum"] = sum_rows(live["first_sum"], "row")[0]

        def cross_terms():
            out_first, own_second = outs(0, count_first), owns(count_first, len(pieces))
            sums = core_sum(lambda odd: dot_tn(out_first, by_parity(own_second, odd), three_pass)
                            + by_parity(live["link_cross"], odd))
            live["cross_sum"] = sum_step(by_rows(sums), "row", 1)

        def cross_rows():
            live["cross_sum"] = sum_rows(live["cross_sum"], "row", 2)[0]

        def cross_cols():
            live["cross_sum"] = rest_of_cols(live["cross_sum"])

        def second_terms():
            out_second, own_second = outs(count_first, len(pieces)), owns(count_first, len(pieces))

            def terms(odd):
                return dot_tn(out_second, by_parity(own_second, odd), three_pass) + by_parity(live["link_second"], odd)

            live["second_sum"] = by_rows(rest_of_cols(core_sum(terms)))

        def second_rows():
            live["second_sum"] = sum_rows(live["second_sum"], "row")[0]

        at(1, link_terms)
        last = len(pieces) - 1 + stages
        for k in range(len(pieces)):
            at(k + stages, lambda k=k: collect(k))
            for step in range(1, cols_axis.bit_length() - 1):
                at(k + stages + step, lambda k=k: spread(k))
        for k in range(len(pieces)):
            at(k + stages + 1, lambda k=k: add_core(k))
            at(k + stages, lambda k=k: multiply(k))
        for k in range(len(pieces)):
            at(k + stages + 1, lambda k=k: add_rest(k))
        end = last + 3
        at(last + 1, cross_terms, first_terms)
        at(last + 2, cross_rows, second_terms, first_rows)
        at(end, second_rows, cross_cols)

        for slot in range(end + 1):
            if slot > 0:
                live = dict(zip(live, lax.optimization_barrier(list(live.values()))))
            for step in slots[slot]:
                step()

        ancestor = jnp.stack([outs(0, count_first), outs(count_first, len(pieces))])
        diagonal = jnp.stack([given_first - live["first_sum"], given_second - live["second_sum"]])
        return ancestor, diagonal, -live["cross_sum"]

    results = [one_pair(panels[s], kept_rows[s, 0, :, None], kept_rows[s, 1, :, None], link_panel[s],
                        diag_inverse[s, 0], diag_inverse[s, 1])
               for s in range(siblings)]
    return tuple(jnp.stack(group) for group in zip(*results))


def solution(mesh):
    in_specs = (
        P(("hyp", "row"), "col"),
        P("hyp", None, ("col", "row"), None),
        P("hyp", None, None),
        P("hyp", None, "row", "col"),
        P(),
    )
    out_specs = (
        P("hyp", None, ("row", "col"), None),
        P("hyp", None, "row", "col"),
        P("hyp", "row", "col"),
    )
    return jax.shard_map(local, mesh=mesh, in_specs=in_specs, out_specs=out_specs, check_vma=False)
```

```python
import jax
import jax.numpy as jnp
from jax import lax
from jax.experimental import pallas as pl
from jax.experimental.pallas import tpu as pltpu
from jax.sharding import PartitionSpec as P

TILE = 128

precise = lax.Precision.HIGHEST
three_pass = lax.Precision.HIGH


def swap(block, axis, bit):
    pairs = [(i, i ^ bit) for i in range(lax.axis_size(axis))]
    return lax.ppermute(block, axis, pairs)


def parts(values):
    high = values.astype(jnp.bfloat16)
    return high, (values - high.astype(jnp.float32)).astype(jnp.bfloat16)


PARTS = 6


def split_kernel(tile_ref, parts_ref):
    parts_ref[0], parts_ref[1] = parts(tile_ref[...])


def split(tile):
    rows, width = tile.shape
    step = min(rows, 256)
    return pl.pallas_call(
        split_kernel,
        grid=(rows // step,),
        in_specs=[pl.BlockSpec((step, width), lambda t: (t, 0))],
        out_specs=pl.BlockSpec((2, step, width), lambda t: (0, t, 0)),
        out_shape=jax.ShapeDtypeStruct((PARTS, rows, width), jnp.bfloat16),
        compiler_params=pltpu.CompilerParams(vmem_limit_bytes=24 * 2**20),
    )(tile)


def product_kernel(place, tile_ref, *refs):
    *block_refs, send_ref, keep_ref, high_ref, low_ref, held, arrived = refs
    height = block_refs[0].shape[0]
    half = send_ref.shape[0]

    def fetch(i, run):
        slot = i % 2
        for part in range(2):
            run(pltpu.make_async_copy(tile_ref.at[part, place[1 + i]], held.at[part, slot], arrived.at[part, slot]))

    fetch(0, lambda copy: copy.start())
    for j, block_ref in enumerate(block_refs):
        rows = pl.ds(pl.multiple_of((place[0] ^ j) * height, height), height)
        high_ref[rows], low_ref[rows] = parts(block_ref[...])

    def times(a, b_ref):
        return jnp.dot(a, b_ref[...], preferred_element_type=jnp.float32)

    for base, out_ref in ((0, send_ref), (half, keep_ref)):
        def step(i, carry):
            @pl.when(base + i + 1 < 2 * half)
            def _():
                fetch(base + i + 1, lambda copy: copy.start())

            fetch(base + i, lambda copy: copy.wait())
            high, low = held[0, (base + i) % 2], held[1, (base + i) % 2]
            out_ref[i] = times(high, high_ref) + (times(high, low_ref) + times(low, high_ref))
            return carry

        lax.fori_loop(0, half, step, 0)


def product(tile, blocks):
    _, count, out_rows, width = tile.shape
    columns = blocks[0].shape[1]
    half = count // 2
    chunks = lax.axis_index("col") ^ jnp.concatenate([2 * jnp.arange(half) + 1, 2 * jnp.arange(half)])
    place = jnp.concatenate([lax.axis_index("row")[None], chunks]).astype(jnp.int32)
    vmem, hbm = (pl.BlockSpec(memory_space=space) for space in (pltpu.VMEM, pltpu.HBM))
    return pl.pallas_call(
        product_kernel,
        in_specs=[pl.BlockSpec(memory_space=pltpu.SMEM), hbm] + [vmem] * len(blocks),
        out_specs=[vmem, vmem],
        out_shape=[jax.ShapeDtypeStruct((half, out_rows, columns), jnp.float32)] * 2,
        scratch_shapes=[pltpu.VMEM((width, columns), jnp.bfloat16)] * 2
        + [pltpu.VMEM((2, 2, out_rows, width), jnp.bfloat16), pltpu.SemaphoreType.DMA((2, 2))],
        compiler_params=pltpu.CompilerParams(vmem_limit_bytes=24 * 2**20),
    )(place, tile, *blocks)


def dot(a, b, precision):
    return jnp.matmul(a, b, precision=precision)


def dot_tn(a, b, precision):
    return lax.dot_general(a, b, (((0,), (0,)), ((), ())), precision=precision)


def sum_scatter(blocks, axis, bit=1):
    while blocks.shape[0] > 1:
        pairs = blocks.reshape((blocks.shape[0] // 2, 2) + blocks.shape[1:])
        blocks = pairs[:, 0] + swap(pairs[:, 1], axis, bit)
        bit *= 2
    return blocks[0]


def sum_step(blocks, axis, bit):
    mine = lax.axis_index(axis) // bit % 2
    pairs = blocks.reshape((blocks.shape[0] // 2, 2) + blocks.shape[1:])
    keep = lax.dynamic_index_in_dim(pairs, mine, 1, keepdims=False)
    return keep + swap(lax.dynamic_index_in_dim(pairs, 1 - mine, 1, keepdims=False), axis, bit)


def sum_rows(blocks, axis, bit=1):
    while blocks.shape[0] > 1:
        blocks = sum_step(blocks, axis, bit)
        bit *= 2
    return blocks[0]


def columns_by_xor(array, odd):
    cols, col_id = lax.axis_size("col"), lax.axis_index("col")
    span = array.shape[1] // cols
    return [lax.dynamic_slice_in_dim(array, (col_id ^ j) * span, span, 1) for j in range(odd, cols, 2)]


def source_col(row):
    return row * lax.axis_size("col") // lax.axis_size("row")


def blocks_to_send(blocks):
    rows, cols = lax.axis_size("row"), lax.axis_size("col")
    held = []
    for d in range(cols):
        wanted = [((r * cols + (source_col(r) ^ d)) % rows) ^ r for r in range(rows)]
        if len(set(wanted)) == 1:
            held.append(blocks[wanted[0]])
        else:
            held.append(lax.dynamic_index_in_dim(jnp.stack(blocks), jnp.array(wanted)[lax.axis_index("row")], 0, keepdims=False))
    return held


def spread_step(held):
    rows, cols = lax.axis_size("row"), lax.axis_size("col")
    bit = len(held) // 2
    pairs = [(r * cols + c, r * cols + (c ^ bit)) for r in range(rows) for c in range(cols)
             if (c ^ source_col(r)) % (2 * bit) == 0]
    moved = lax.ppermute(jnp.stack(held[bit:]), ("row", "col"), pairs)
    offset = lax.axis_index("col") ^ source_col(lax.axis_index("row"))
    return [jnp.where(offset & bit != 0, moved[j], held[j]) for j in range(bit)]


def local(inverse_tile, panels, link_panel, diag_inverse, ancestor_tiles):
    rows_axis, cols_axis = lax.axis_size("row"), lax.axis_size("col")
    row_id, col_id = lax.axis_index("row"), lax.axis_index("col")
    siblings, _, local_rows, width = panels.shape
    height, span = diag_inverse.shape[2:]
    row_start = (col_id * rows_axis + row_id) * local_rows
    tile_mask = jnp.repeat(ancestor_tiles, TILE, axis=2)
    kept_rows = lax.dynamic_slice_in_dim(tile_mask, row_start, local_rows, 2).astype(jnp.float32)
    tile = split(inverse_tile).reshape(PARTS, cols_axis, -1, inverse_tile.shape[1])

    def one_pair(panels, kept_first, kept_second, link, given_first, given_second):
        live = {"tile": tile, "given": given_first}
        slots = {}

        def at(slot, *steps):
            slots.setdefault(slot, []).extend(steps)

        late = 2 * span
        pieces = [("first", i, i + late) for i in range(0, width, late)]
        count_first = len(pieces)
        pieces += [("second", i, i + late) for i in range(0, width, late)]
        stages = rows_axis.bit_length() - 1
        second = panels[1] * kept_second - dot(panels[0] * kept_first, link, precise)
        for k, (panel, start, stop) in enumerate(pieces):
            live["piece", k] = panels[0][:, start:stop] * kept_first if panel == "first" else second[:, start:stop]

        def fetch(k, stage):
            if stage == 0:
                live[k, 0] = live.pop(("piece", k))
            for j in reversed(range(1, rows_axis)):
                if j.bit_count() == stage + 1:
                    live[k, j] = swap(live[k, j & (j - 1)], "row", j & -j)

        def blocks(k):
            return [live[k, j] for j in range(rows_axis)]

        def multiply(k):
            gathered = blocks(k)
            if ("sums", k - 1) in live and k + stages >= len(pieces):
                live["sums", k - 1], gathered = lax.optimization_barrier((live["sums", k - 1], gathered))
            live["send", k], live["keep", k] = product(live["tile"], gathered)

        def add_core(k):
            live["sums", k] = live.pop(("keep", k)) + swap(live.pop(("send", k)), "col", 1)

        def add_rest(k):
            live["out", k] = -sum_scatter(live.pop(("sums", k)), "col", 2)

        def collect(group):
            live["own", group] = blocks_to_send([jnp.concatenate(parts, axis=1) for parts in zip(*map(blocks, group))])
            spread(group)

        def spread(group):
            live["own", group] = spread_step(live["own", group])

        own_groups = [tuple(range(count_first))] + [(k,) for k in range(count_first, len(pieces))]

        def owns(groups):
            return jnp.concatenate([live["own", group][0] for group in groups], axis=1)

        def outs(start, stop):
            return jnp.concatenate([live["out", k] for k in range(start, stop)], axis=1)

        for k in range(len(pieces)):
            for stage in range(stages):
                at(k + stage, lambda k=k, stage=stage: fetch(k, stage))

        def link_terms():
            link_rows = lax.dynamic_slice_in_dim(link, row_id * height, height, 0)
            link_cols = lax.dynamic_slice_in_dim(link, col_id * span, span, 0)
            given = dot(live["given"], link_cols, precise)
            live["link_cross"] = lax.dynamic_update_slice_in_dim(jnp.zeros_like(link), given, row_id * height, 0)
            live["link_second"] = -dot_tn(link_rows, given, precise)

        def core_sum(terms):
            sent = swap(terms(1), "col", 1)
            return terms(0) + sent

        def by_rows(sums):
            return sums.reshape(-1, rows_axis, height, sums.shape[1]).swapaxes(0, 1)

        def rest_of_cols(sums):
            return sum_scatter(sums.reshape(-1, cols_axis // 2, span).swapaxes(0, 1), "col", 2)

        def by_parity(array, odd):
            return jnp.concatenate(columns_by_xor(array, odd), axis=1)

        def first_terms():
            out_first, own_first = outs(0, count_first), owns(own_groups[:1])
            sums = core_sum(lambda odd: dot_tn(out_first, by_parity(own_first, odd), three_pass))
            live["first_sum"] = by_rows(sums)

        def first_rows():
            live["first_sum"] = sum_rows(live["first_sum"], "row")[0]

        def first_cols():
            live["first_sum"] = rest_of_cols(live["first_sum"])

        def cross_terms():
            out_first, own_second = outs(0, count_first), owns(own_groups[1:])
            sums = core_sum(lambda odd: dot_tn(out_first, by_parity(own_second, odd), three_pass)
                            + by_parity(live["link_cross"], odd))
            live["cross_sum"] = sum_step(by_rows(sums), "row", 1)

        def cross_rest():
            live["cross_sum"] = rest_of_cols(sum_rows(live["cross_sum"], "row", 2)[0])

        def second_terms():
            out_second, own_second = outs(count_first, len(pieces)), owns(own_groups[1:])

            def terms(odd):
                return dot_tn(out_second, by_parity(own_second, odd), three_pass) + by_parity(live["link_second"], odd)

            live["second_sum"] = sum_rows(by_rows(rest_of_cols(core_sum(terms))), "row")[0]

        at(1, link_terms)
        last = len(pieces) - 1 + stages
        for group in own_groups:
            at(group[-1] + stages, lambda group=group: collect(group))
            for step in range(1, cols_axis.bit_length() - 1):
                at(group[-1] + stages + step, lambda group=group: spread(group))
        for k in range(len(pieces)):
            at(k + stages + 1, lambda k=k: add_core(k))
            at(k + stages, lambda k=k: multiply(k))
        for k in range(len(pieces)):
            at(k + stages + 1, lambda k=k: add_rest(k))
        end = last + 2
        at(last, first_terms)
        at(last + 1, cross_terms, first_rows)
        at(end, cross_rest, second_terms, first_cols)

        for slot in range(end + 1):
            if slot > 0:
                live = dict(zip(live, lax.optimization_barrier(list(live.values()))))
            for step in slots[slot]:
                step()

        ancestor = jnp.stack([outs(0, count_first), outs(count_first, len(pieces))])
        diagonal = jnp.stack([given_first - live["first_sum"], given_second - live["second_sum"]])
        return ancestor, diagonal, -live["cross_sum"]

    results = [one_pair(panels[s], kept_rows[s, 0, :, None], kept_rows[s, 1, :, None], link_panel[s],
                        diag_inverse[s, 0], diag_inverse[s, 1])
               for s in range(siblings)]
    return tuple(jnp.stack(group) for group in zip(*results))


def solution(mesh):
    in_specs = (
        P(("hyp", "row"), "col"),
        P("hyp", None, ("col", "row"), None),
        P("hyp", None, None),
        P("hyp", None, "row", "col"),
        P(),
    )
    out_specs = (
        P("hyp", None, ("row", "col"), None),
        P("hyp", None, "row", "col"),
        P("hyp", "row", "col"),
    )
    return jax.shard_map(local, mesh=mesh, in_specs=in_specs, out_specs=out_specs, check_vma=False)
```

```python
import jax
import jax.numpy as jnp
from jax import lax
from jax.experimental import pallas as pl
from jax.experimental.pallas import tpu as pltpu
from jax.sharding import PartitionSpec as P

TILE = 128

precise = lax.Precision.HIGHEST
three_pass = lax.Precision.HIGH


def swap(block, axis, bit):
    pairs = [(i, i ^ bit) for i in range(lax.axis_size(axis))]
    return lax.ppermute(block, axis, pairs)


def parts(values):
    high = values.astype(jnp.bfloat16)
    return high, (values - high.astype(jnp.float32)).astype(jnp.bfloat16)


PARTS = 6


def split_kernel(tile_ref, parts_ref):
    parts_ref[0], parts_ref[1] = parts(tile_ref[...])


def split(tile):
    rows, width = tile.shape
    step = min(rows, 256)
    return pl.pallas_call(
        split_kernel,
        grid=(rows // step,),
        in_specs=[pl.BlockSpec((step, width), lambda t: (t, 0))],
        out_specs=pl.BlockSpec((2, step, width), lambda t: (0, t, 0)),
        out_shape=jax.ShapeDtypeStruct((PARTS, rows, width), jnp.bfloat16),
        compiler_params=pltpu.CompilerParams(vmem_limit_bytes=24 * 2**20),
    )(tile)


def product_kernel(place, tile_ref, *refs):
    *block_refs, send_ref, keep_ref, high_ref, low_ref, held, arrived = refs
    height = block_refs[0].shape[0]
    half = send_ref.shape[0]

    def fetch(i, run):
        slot = i % 2
        for part in range(2):
            run(pltpu.make_async_copy(tile_ref.at[part, place[1 + i]], held.at[part, slot], arrived.at[part, slot]))

    fetch(0, lambda copy: copy.start())
    for j, block_ref in enumerate(block_refs):
        rows = pl.ds(pl.multiple_of((place[0] ^ j) * height, height), height)
        high_ref[rows], low_ref[rows] = parts(block_ref[...])

    def times(a, b_ref):
        return jnp.dot(a, b_ref[...], preferred_element_type=jnp.float32)

    for base, out_ref in ((0, send_ref), (half, keep_ref)):
        def step(i, carry):
            @pl.when(base + i + 1 < 2 * half)
            def _():
                fetch(base + i + 1, lambda copy: copy.start())

            fetch(base + i, lambda copy: copy.wait())
            high, low = held[0, (base + i) % 2], held[1, (base + i) % 2]
            out_ref[i] = times(high, high_ref) + (times(high, low_ref) + times(low, high_ref))
            return carry

        lax.fori_loop(0, half, step, 0)


def product(tile, blocks):
    _, count, out_rows, width = tile.shape
    columns = blocks[0].shape[1]
    half = count // 2
    chunks = lax.axis_index("col") ^ jnp.concatenate([2 * jnp.arange(half) + 1, 2 * jnp.arange(half)])
    place = jnp.concatenate([lax.axis_index("row")[None], chunks]).astype(jnp.int32)
    vmem, hbm = (pl.BlockSpec(memory_space=space) for space in (pltpu.VMEM, pltpu.HBM))
    return pl.pallas_call(
        product_kernel,
        in_specs=[pl.BlockSpec(memory_space=pltpu.SMEM), hbm] + [vmem] * len(blocks),
        out_specs=[vmem, vmem],
        out_shape=[jax.ShapeDtypeStruct((half, out_rows, columns), jnp.float32)] * 2,
        scratch_shapes=[pltpu.VMEM((width, columns), jnp.bfloat16)] * 2
        + [pltpu.VMEM((2, 2, out_rows, width), jnp.bfloat16), pltpu.SemaphoreType.DMA((2, 2))],
        compiler_params=pltpu.CompilerParams(vmem_limit_bytes=24 * 2**20),
    )(place, tile, *blocks)


def dot(a, b, precision):
    return jnp.matmul(a, b, precision=precision)


def dot_tn(a, b, precision):
    return lax.dot_general(a, b, (((0,), (0,)), ((), ())), precision=precision)


def sum_scatter(blocks, axis, bit=1):
    while blocks.shape[0] > 1:
        pairs = blocks.reshape((blocks.shape[0] // 2, 2) + blocks.shape[1:])
        blocks = pairs[:, 0] + swap(pairs[:, 1], axis, bit)
        bit *= 2
    return blocks[0]


def sum_step(blocks, axis, bit):
    mine = lax.axis_index(axis) // bit % 2
    pairs = blocks.reshape((blocks.shape[0] // 2, 2) + blocks.shape[1:])
    keep = lax.dynamic_index_in_dim(pairs, mine, 1, keepdims=False)
    return keep + swap(lax.dynamic_index_in_dim(pairs, 1 - mine, 1, keepdims=False), axis, bit)


def sum_rows(blocks, axis, bit=1):
    while blocks.shape[0] > 1:
        blocks = sum_step(blocks, axis, bit)
        bit *= 2
    return blocks[0]


def columns_by_xor(array, odd):
    cols, col_id = lax.axis_size("col"), lax.axis_index("col")
    span = array.shape[1] // cols
    return [lax.dynamic_slice_in_dim(array, (col_id ^ j) * span, span, 1) for j in range(odd, cols, 2)]


def source_col(row):
    return row * lax.axis_size("col") // lax.axis_size("row")


def blocks_to_send(blocks):
    rows, cols = lax.axis_size("row"), lax.axis_size("col")
    held = []
    for d in range(cols):
        wanted = [((r * cols + (source_col(r) ^ d)) % rows) ^ r for r in range(rows)]
        if len(set(wanted)) == 1:
            held.append(blocks[wanted[0]])
        else:
            held.append(lax.dynamic_index_in_dim(jnp.stack(blocks), jnp.array(wanted)[lax.axis_index("row")], 0, keepdims=False))
    return held


def spread_step(held):
    bit = len(held) // 2
    moved = swap(jnp.stack(held[bit:]), "col", bit)
    offset = lax.axis_index("col") ^ source_col(lax.axis_index("row"))
    return [jnp.where(offset & bit != 0, moved[j], held[j]) for j in range(bit)]


def local(inverse_tile, panels, link_panel, diag_inverse, ancestor_tiles):
    rows_axis, cols_axis = lax.axis_size("row"), lax.axis_size("col")
    row_id, col_id = lax.axis_index("row"), lax.axis_index("col")
    siblings, _, local_rows, width = panels.shape
    height, span = diag_inverse.shape[2:]
    row_start = (col_id * rows_axis + row_id) * local_rows
    tile_mask = jnp.repeat(ancestor_tiles, TILE, axis=2)
    kept_rows = lax.dynamic_slice_in_dim(tile_mask, row_start, local_rows, 2).astype(jnp.float32)
    tile = split(inverse_tile).reshape(PARTS, cols_axis, -1, inverse_tile.shape[1])

    def one_pair(panels, kept_first, kept_second, link, given_first, given_second):
        live = {"tile": tile, "given": given_first}
        slots = {}

        def at(slot, *steps):
            slots.setdefault(slot, []).extend(steps)

        late = 2 * span
        pieces = [("first", i, i + late) for i in range(0, width, late)]
        count_first = len(pieces)
        pieces += [("second", i, i + late) for i in range(0, width, late)]
        stages = rows_axis.bit_length() - 1
        second = panels[1] * kept_second - dot(panels[0] * kept_first, link, precise)
        for k, (panel, start, stop) in enumerate(pieces):
            live["piece", k] = panels[0][:, start:stop] * kept_first if panel == "first" else second[:, start:stop]

        def fetch(k, stage):
            if stage == 0:
                live[k, 0] = live.pop(("piece", k))
            for j in reversed(range(1, rows_axis)):
                if j.bit_count() == stage + 1:
                    live[k, j] = swap(live[k, j & (j - 1)], "row", j & -j)

        def blocks(k):
            return [live[k, j] for j in range(rows_axis)]

        def multiply(k):
            gathered = blocks(k)
            if ("sums", k - 1) in live:
                live["sums", k - 1], gathered = lax.optimization_barrier((live["sums", k - 1], gathered))
            live["send", k], live["keep", k] = product(live["tile"], gathered)

        def add_core(k):
            live["sums", k] = live.pop(("keep", k)) + swap(live.pop(("send", k)), "col", 1)

        def add_rest(k):
            live["out", k] = -sum_scatter(live.pop(("sums", k)), "col", 2)

        def collect(k):
            live["own", k] = blocks_to_send(blocks(k))
            spread(k)

        def spread(k):
            live["own", k] = spread_step(live["own", k])

        def owns(start, stop):
            return jnp.concatenate([live["own", k][0] for k in range(start, stop)], axis=1)

        def outs(start, stop):
            return jnp.concatenate([live["out", k] for k in range(start, stop)], axis=1)

        for k in range(len(pieces)):
            for stage in range(stages):
                at(k + stage, lambda k=k, stage=stage: fetch(k, stage))

        def link_terms():
            link_rows = lax.dynamic_slice_in_dim(link, row_id * height, height, 0)
            link_cols = lax.dynamic_slice_in_dim(link, col_id * span, span, 0)
            given = dot(live["given"], link_cols, precise)
            live["link_cross"] = lax.dynamic_update_slice_in_dim(jnp.zeros_like(link), given, row_id * height, 0)
            live["link_second"] = -dot_tn(link_rows, given, precise)

        def core_sum(terms):
            sent = swap(terms(1), "col", 1)
            return terms(0) + sent

        def by_rows(sums):
            return sums.reshape(-1, rows_axis, height, sums.shape[1]).swapaxes(0, 1)

        def rest_of_cols(sums):
            return sum_scatter(sums.reshape(-1, cols_axis // 2, span).swapaxes(0, 1), "col", 2)

        def by_parity(array, odd):
            return jnp.concatenate(columns_by_xor(array, odd), axis=1)

        def first_terms():
            out_first = outs(0, count_first)
            own_first, own_second = owns(0, count_first), owns(count_first, len(pieces))

            def terms(odd):
                cross = dot_tn(out_first, by_parity(own_second, odd), three_pass) + by_parity(live["link_cross"], odd)
                return jnp.concatenate([dot_tn(out_first, by_parity(own_first, odd), three_pass), cross])

            live["first_sums"] = sum_step(by_rows(core_sum(terms)), "row", 1)

        def first_sums():
            sums = sum_rows(live["first_sums"], "row", 2)
            live["first_sums"] = rest_of_cols(sums.reshape(-1, sums.shape[2])).reshape(-1, height, span)

        def second_terms():
            out_second, own_second = outs(count_first, len(pieces)), owns(count_first, len(pieces))

            def terms(odd):
                return dot_tn(out_second, by_parity(own_second, odd), three_pass) + by_parity(live["link_second"], odd)

            live["second_sum"] = sum_rows(by_rows(rest_of_cols(core_sum(terms))), "row")[0]

        at(1, link_terms)
        last = len(pieces) - 1 + stages
        for k in range(len(pieces)):
            at(k + stages, lambda k=k: collect(k))
            for step in range(1, cols_axis.bit_length() - 1):
                at(k + stages + step, lambda k=k: spread(k))
        for k in range(len(pieces)):
            at(k + stages + 1, lambda k=k: add_core(k))
            at(k + stages, lambda k=k: multiply(k))
        for k in range(len(pieces)):
            at(k + stages + 1, lambda k=k: add_rest(k))
        end = last + 2
        at(last + 1, first_terms)
        at(end, first_sums, second_terms)

        for slot in range(end + 1):
            if slot > 0:
                live = dict(zip(live, lax.optimization_barrier(list(live.values()))))
            for step in slots[slot]:
                step()

        first_sum, cross_sum = live["first_sums"]
        ancestor = jnp.stack([outs(0, count_first), outs(count_first, len(pieces))])
        diagonal = jnp.stack([given_first - first_sum, given_second - live["second_sum"]])
        return ancestor, diagonal, -cross_sum

    results = [one_pair(panels[s], kept_rows[s, 0, :, None], kept_rows[s, 1, :, None], link_panel[s],
                        diag_inverse[s, 0], diag_inverse[s, 1])
               for s in range(siblings)]
    return tuple(jnp.stack(group) for group in zip(*results))


def solution(mesh):
    in_specs = (
        P(("hyp", "row"), "col"),
        P("hyp", None, ("col", "row"), None),
        P("hyp", None, None),
        P("hyp", None, "row", "col"),
        P(),
    )
    out_specs = (
        P("hyp", None, ("row", "col"), None),
        P("hyp", None, "row", "col"),
        P("hyp", "row", "col"),
    )
    return jax.shard_map(local, mesh=mesh, in_specs=in_specs, out_specs=out_specs, check_vma=False)
```

```python
import jax
import jax.numpy as jnp
from jax import lax
from jax.experimental import pallas as pl
from jax.experimental.pallas import tpu as pltpu
from jax.sharding import PartitionSpec as P

TILE = 128

precise = lax.Precision.HIGHEST
three_pass = lax.Precision.HIGH


def swap(block, axis, bit):
    pairs = [(i, i ^ bit) for i in range(lax.axis_size(axis))]
    return lax.ppermute(block, axis, pairs)


def parts(values):
    high = values.astype(jnp.bfloat16)
    return high, (values - high.astype(jnp.float32)).astype(jnp.bfloat16)


PARTS = 6


def split_kernel(tile_ref, parts_ref):
    parts_ref[0], parts_ref[1] = parts(tile_ref[...])


def split(tile):
    rows, width = tile.shape
    step = min(rows, 256)
    return pl.pallas_call(
        split_kernel,
        grid=(rows // step,),
        in_specs=[pl.BlockSpec((step, width), lambda t: (t, 0))],
        out_specs=pl.BlockSpec((2, step, width), lambda t: (0, t, 0)),
        out_shape=jax.ShapeDtypeStruct((PARTS, rows, width), jnp.bfloat16),
        compiler_params=pltpu.CompilerParams(vmem_limit_bytes=24 * 2**20),
    )(tile)


def product_kernel(place, tile_ref, *refs):
    *block_refs, send_ref, keep_ref, high_ref, low_ref, held, arrived = refs
    height = block_refs[0].shape[0]
    half = send_ref.shape[0]

    def fetch(i, run):
        slot = i % 2
        for part in range(2):
            run(pltpu.make_async_copy(tile_ref.at[part, place[1 + i]], held.at[part, slot], arrived.at[part, slot]))

    fetch(0, lambda copy: copy.start())
    for j, block_ref in enumerate(block_refs):
        rows = pl.ds(pl.multiple_of((place[0] ^ j) * height, height), height)
        high_ref[rows], low_ref[rows] = parts(block_ref[...])

    def times(a, b_ref):
        return jnp.dot(a, b_ref[...], preferred_element_type=jnp.float32)

    for base, out_ref in ((0, send_ref), (half, keep_ref)):
        def step(i, carry):
            @pl.when(base + i + 1 < 2 * half)
            def _():
                fetch(base + i + 1, lambda copy: copy.start())

            fetch(base + i, lambda copy: copy.wait())
            high, low = held[0, (base + i) % 2], held[1, (base + i) % 2]
            out_ref[i] = times(high, high_ref) + (times(high, low_ref) + times(low, high_ref))
            return carry

        lax.fori_loop(0, half, step, 0)


def product(tile, blocks):
    _, count, out_rows, width = tile.shape
    columns = blocks[0].shape[1]
    half = count // 2
    chunks = lax.axis_index("col") ^ jnp.concatenate([2 * jnp.arange(half) + 1, 2 * jnp.arange(half)])
    place = jnp.concatenate([lax.axis_index("row")[None], chunks]).astype(jnp.int32)
    vmem, hbm = (pl.BlockSpec(memory_space=space) for space in (pltpu.VMEM, pltpu.HBM))
    return pl.pallas_call(
        product_kernel,
        in_specs=[pl.BlockSpec(memory_space=pltpu.SMEM), hbm] + [vmem] * len(blocks),
        out_specs=[vmem, vmem],
        out_shape=[jax.ShapeDtypeStruct((half, out_rows, columns), jnp.float32)] * 2,
        scratch_shapes=[pltpu.VMEM((width, columns), jnp.bfloat16)] * 2
        + [pltpu.VMEM((2, 2, out_rows, width), jnp.bfloat16), pltpu.SemaphoreType.DMA((2, 2))],
        compiler_params=pltpu.CompilerParams(vmem_limit_bytes=24 * 2**20),
    )(place, tile, *blocks)


def dot(a, b, precision):
    return jnp.matmul(a, b, precision=precision)


def dot_tn(a, b, precision):
    return lax.dot_general(a, b, (((0,), (0,)), ((), ())), precision=precision)


def sum_scatter(blocks, axis, bit=1):
    while blocks.shape[0] > 1:
        pairs = blocks.reshape((blocks.shape[0] // 2, 2) + blocks.shape[1:])
        blocks = pairs[:, 0] + swap(pairs[:, 1], axis, bit)
        bit *= 2
    return blocks[0]


def sum_step(blocks, axis, bit):
    mine = lax.axis_index(axis) // bit % 2
    pairs = blocks.reshape((blocks.shape[0] // 2, 2) + blocks.shape[1:])
    keep = lax.dynamic_index_in_dim(pairs, mine, 1, keepdims=False)
    return keep + swap(lax.dynamic_index_in_dim(pairs, 1 - mine, 1, keepdims=False), axis, bit)


def sum_rows(blocks, axis, bit=1):
    while blocks.shape[0] > 1:
        blocks = sum_step(blocks, axis, bit)
        bit *= 2
    return blocks[0]


def columns_by_xor(array, odd):
    cols, col_id = lax.axis_size("col"), lax.axis_index("col")
    span = array.shape[1] // cols
    return [lax.dynamic_slice_in_dim(array, (col_id ^ j) * span, span, 1) for j in range(odd, cols, 2)]


def source_col(row):
    return row * lax.axis_size("col") // lax.axis_size("row")


def blocks_to_send(blocks):
    rows, cols = lax.axis_size("row"), lax.axis_size("col")
    held = []
    for d in range(cols):
        wanted = [((r * cols + (source_col(r) ^ d)) % rows) ^ r for r in range(rows)]
        if len(set(wanted)) == 1:
            held.append(blocks[wanted[0]])
        else:
            held.append(lax.dynamic_index_in_dim(jnp.stack(blocks), jnp.array(wanted)[lax.axis_index("row")], 0, keepdims=False))
    return held


def spread_step(held, one_way=False):
    rows, cols = lax.axis_size("row"), lax.axis_size("col")
    bit = len(held) // 2
    if one_way:
        pairs = [(r * cols + c, r * cols + (c ^ bit)) for r in range(rows) for c in range(cols)
                 if (c ^ source_col(r)) % (2 * bit) == 0]
        moved = lax.ppermute(jnp.stack(held[bit:]), ("row", "col"), pairs)
    else:
        moved = swap(jnp.stack(held[bit:]), "col", bit)
    offset = lax.axis_index("col") ^ source_col(lax.axis_index("row"))
    return [jnp.where(offset & bit != 0, moved[j], held[j]) for j in range(bit)]


def local(inverse_tile, panels, link_panel, diag_inverse, ancestor_tiles):
    rows_axis, cols_axis = lax.axis_size("row"), lax.axis_size("col")
    row_id, col_id = lax.axis_index("row"), lax.axis_index("col")
    siblings, _, local_rows, width = panels.shape
    height, span = diag_inverse.shape[2:]
    row_start = (col_id * rows_axis + row_id) * local_rows
    tile_mask = jnp.repeat(ancestor_tiles, TILE, axis=2)
    kept_rows = lax.dynamic_slice_in_dim(tile_mask, row_start, local_rows, 2).astype(jnp.float32)
    tile = split(inverse_tile).reshape(PARTS, cols_axis, -1, inverse_tile.shape[1])

    def one_pair(panels, kept_first, kept_second, link, given_first, given_second):
        live = {"tile": tile, "given": given_first}
        slots = {}

        def at(slot, *steps):
            slots.setdefault(slot, []).extend(steps)

        late = 2 * span
        pieces = [("first", i, i + late) for i in range(0, width, late)]
        count_first = len(pieces)
        pieces += [("second", i, i + late) for i in range(0, width, late)]
        stages = rows_axis.bit_length() - 1
        second = panels[1] * kept_second - dot(panels[0] * kept_first, link, precise)
        for k, (panel, start, stop) in enumerate(pieces):
            live["piece", k] = panels[0][:, start:stop] * kept_first if panel == "first" else second[:, start:stop]

        def fetch(k, stage):
            if stage == 0:
                live[k, 0] = live.pop(("piece", k))
            for j in reversed(range(1, rows_axis)):
                if j.bit_count() == stage + 1:
                    live[k, j] = swap(live[k, j & (j - 1)], "row", j & -j)

        def blocks(k):
            return [live[k, j] for j in range(rows_axis)]

        def multiply(k):
            gathered = blocks(k)
            if ("sums", k - 1) in live:
                live["sums", k - 1], gathered = lax.optimization_barrier((live["sums", k - 1], gathered))
            live["send", k], live["keep", k] = product(live["tile"], gathered)

        def add_core(k):
            live["sums", k] = live.pop(("keep", k)) + swap(live.pop(("send", k)), "col", 1)

        def add_rest(k):
            live["out", k] = -sum_scatter(live.pop(("sums", k)), "col", 2)

        def collect(k):
            live["own", k] = spread_step(blocks_to_send(blocks(k)), one_way=k >= count_first)

        def spread(k):
            live["own", k] = spread_step(live["own", k])

        def owns(start, stop):
            return jnp.concatenate([live["own", k][0] for k in range(start, stop)], axis=1)

        def outs(start, stop):
            return jnp.concatenate([live["out", k] for k in range(start, stop)], axis=1)

        for k in range(len(pieces)):
            for stage in range(stages):
                at(k + stage, lambda k=k, stage=stage: fetch(k, stage))

        def link_terms():
            link_rows = lax.dynamic_slice_in_dim(link, row_id * height, height, 0)
            link_cols = lax.dynamic_slice_in_dim(link, col_id * span, span, 0)
            given = dot(live["given"], link_cols, precise)
            live["link_cross"] = lax.dynamic_update_slice_in_dim(jnp.zeros_like(link), given, row_id * height, 0)
            live["link_second"] = -dot_tn(link_rows, given, precise)

        def core_sum(terms):
            sent = swap(terms(1), "col", 1)
            return terms(0) + sent

        def by_rows(sums):
            return sums.reshape(-1, rows_axis, height, sums.shape[1]).swapaxes(0, 1)

        def rest_of_cols(sums):
            return sum_scatter(sums.reshape(-1, cols_axis // 2, span).swapaxes(0, 1), "col", 2)

        def by_parity(array, odd):
            return jnp.concatenate(columns_by_xor(array, odd), axis=1)

        def first_terms():
            out_first = outs(0, count_first)
            own_first, own_second = owns(0, count_first), owns(count_first, len(pieces))

            def terms(odd):
                cross = dot_tn(out_first, by_parity(own_second, odd), three_pass) + by_parity(live["link_cross"], odd)
                return jnp.concatenate([dot_tn(out_first, by_parity(own_first, odd), three_pass), cross])

            live["first_sums"] = sum_step(by_rows(core_sum(terms)), "row", 1)

        def first_sums():
            sums = sum_rows(live["first_sums"], "row", 2)
            live["first_sums"] = rest_of_cols(sums.reshape(-1, sums.shape[2])).reshape(-1, height, span)

        def second_terms():
            out_second, own_second = outs(count_first, len(pieces)), owns(count_first, len(pieces))

            def terms(odd):
                return dot_tn(out_second, by_parity(own_second, odd), three_pass) + by_parity(live["link_second"], odd)

            live["second_sum"] = sum_rows(by_rows(rest_of_cols(core_sum(terms))), "row")[0]

        at(1, link_terms)
        last = len(pieces) - 1 + stages
        for k in range(len(pieces)):
            at(k + stages, lambda k=k: collect(k))
            for step in range(1, cols_axis.bit_length() - 1):
                at(k + stages + step, lambda k=k: spread(k))
        for k in range(len(pieces)):
            at(k + stages + 1, lambda k=k: add_core(k))
            at(k + stages, lambda k=k: multiply(k))
        for k in range(len(pieces)):
            at(k + stages + 1, lambda k=k: add_rest(k))
        end = last + 2
        at(last + 1, first_terms)
        at(end, first_sums, second_terms)

        for slot in range(end + 1):
            if slot > 0:
                live = dict(zip(live, lax.optimization_barrier(list(live.values()))))
            for step in slots[slot]:
                step()

        first_sum, cross_sum = live["first_sums"]
        ancestor = jnp.stack([outs(0, count_first), outs(count_first, len(pieces))])
        diagonal = jnp.stack([given_first - first_sum, given_second - live["second_sum"]])
        return ancestor, diagonal, -cross_sum

    results = [one_pair(panels[s], kept_rows[s, 0, :, None], kept_rows[s, 1, :, None], link_panel[s],
                        diag_inverse[s, 0], diag_inverse[s, 1])
               for s in range(siblings)]
    return tuple(jnp.stack(group) for group in zip(*results))


def solution(mesh):
    in_specs = (
        P(("hyp", "row"), "col"),
        P("hyp", None, ("col", "row"), None),
        P("hyp", None, None),
        P("hyp", None, "row", "col"),
        P(),
    )
    out_specs = (
        P("hyp", None, ("row", "col"), None),
        P("hyp", None, "row", "col"),
        P("hyp", "row", "col"),
    )
    return jax.shard_map(local, mesh=mesh, in_specs=in_specs, out_specs=out_specs, check_vma=False)
```

```python
import jax
import jax.numpy as jnp
from jax import lax
from jax.experimental import pallas as pl
from jax.experimental.pallas import tpu as pltpu
from jax.sharding import PartitionSpec as P

TILE = 128

precise = lax.Precision.HIGHEST
three_pass = lax.Precision.HIGH


def swap(block, axis, bit):
    pairs = [(i, i ^ bit) for i in range(lax.axis_size(axis))]
    return lax.ppermute(block, axis, pairs)


def parts(values):
    high = values.astype(jnp.bfloat16)
    return high, (values - high.astype(jnp.float32)).astype(jnp.bfloat16)


PARTS = 6


def split_kernel(tile_ref, parts_ref):
    parts_ref[0], parts_ref[1] = parts(tile_ref[...])


def split(tile):
    rows, width = tile.shape
    step = min(rows, 256)
    return pl.pallas_call(
        split_kernel,
        grid=(rows // step,),
        in_specs=[pl.BlockSpec((step, width), lambda t: (t, 0))],
        out_specs=pl.BlockSpec((2, step, width), lambda t: (0, t, 0)),
        out_shape=jax.ShapeDtypeStruct((PARTS, rows, width), jnp.bfloat16),
        compiler_params=pltpu.CompilerParams(vmem_limit_bytes=24 * 2**20),
    )(tile)


def product_kernel(place, tile_ref, *refs):
    *block_refs, send_ref, keep_ref, high_ref, low_ref, held, arrived = refs
    height = block_refs[0].shape[0]
    half = send_ref.shape[0]

    def fetch(i, run):
        slot = i % 2
        for part in range(2):
            run(pltpu.make_async_copy(tile_ref.at[part, place[1 + i]], held.at[part, slot], arrived.at[part, slot]))

    fetch(0, lambda copy: copy.start())
    for j, block_ref in enumerate(block_refs):
        rows = pl.ds(pl.multiple_of((place[0] ^ j) * height, height), height)
        high_ref[rows], low_ref[rows] = parts(block_ref[...])

    def times(a, b_ref):
        return jnp.dot(a, b_ref[...], preferred_element_type=jnp.float32)

    for base, out_ref in ((0, send_ref), (half, keep_ref)):
        def step(i, carry):
            @pl.when(base + i + 1 < 2 * half)
            def _():
                fetch(base + i + 1, lambda copy: copy.start())

            fetch(base + i, lambda copy: copy.wait())
            high, low = held[0, (base + i) % 2], held[1, (base + i) % 2]
            out_ref[i] = times(high, high_ref) + (times(high, low_ref) + times(low, high_ref))
            return carry

        lax.fori_loop(0, half, step, 0)


def product(tile, blocks):
    _, count, out_rows, width = tile.shape
    columns = blocks[0].shape[1]
    half = count // 2
    chunks = lax.axis_index("col") ^ jnp.concatenate([2 * jnp.arange(half) + 1, 2 * jnp.arange(half)])
    place = jnp.concatenate([lax.axis_index("row")[None], chunks]).astype(jnp.int32)
    vmem, hbm = (pl.BlockSpec(memory_space=space) for space in (pltpu.VMEM, pltpu.HBM))
    return pl.pallas_call(
        product_kernel,
        in_specs=[pl.BlockSpec(memory_space=pltpu.SMEM), hbm] + [vmem] * len(blocks),
        out_specs=[vmem, vmem],
        out_shape=[jax.ShapeDtypeStruct((half, out_rows, columns), jnp.float32)] * 2,
        scratch_shapes=[pltpu.VMEM((width, columns), jnp.bfloat16)] * 2
        + [pltpu.VMEM((2, 2, out_rows, width), jnp.bfloat16), pltpu.SemaphoreType.DMA((2, 2))],
        compiler_params=pltpu.CompilerParams(vmem_limit_bytes=24 * 2**20),
    )(place, tile, *blocks)


def dot(a, b, precision):
    return jnp.matmul(a, b, precision=precision)


def dot_tn(a, b, precision):
    return lax.dot_general(a, b, (((0,), (0,)), ((), ())), precision=precision)


def sum_scatter(blocks, axis, bit=1):
    while blocks.shape[0] > 1:
        pairs = blocks.reshape((blocks.shape[0] // 2, 2) + blocks.shape[1:])
        blocks = pairs[:, 0] + swap(pairs[:, 1], axis, bit)
        bit *= 2
    return blocks[0]


def sum_step(blocks, axis, bit):
    mine = lax.axis_index(axis) // bit % 2
    pairs = blocks.reshape((blocks.shape[0] // 2, 2) + blocks.shape[1:])
    keep = lax.dynamic_index_in_dim(pairs, mine, 1, keepdims=False)
    return keep + swap(lax.dynamic_index_in_dim(pairs, 1 - mine, 1, keepdims=False), axis, bit)


def sum_rows(blocks, axis, bit=1):
    while blocks.shape[0] > 1:
        blocks = sum_step(blocks, axis, bit)
        bit *= 2
    return blocks[0]


def columns_by_xor(array, odd):
    cols, col_id = lax.axis_size("col"), lax.axis_index("col")
    span = array.shape[1] // cols
    return [lax.dynamic_slice_in_dim(array, (col_id ^ j) * span, span, 1) for j in range(odd, cols, 2)]


def source_col(row):
    return row * lax.axis_size("col") // lax.axis_size("row")


def blocks_to_send(blocks):
    rows, cols = lax.axis_size("row"), lax.axis_size("col")
    held = []
    for d in range(cols):
        wanted = [((r * cols + (source_col(r) ^ d)) % rows) ^ r for r in range(rows)]
        if len(set(wanted)) == 1:
            held.append(blocks[wanted[0]])
        else:
            held.append(lax.dynamic_index_in_dim(jnp.stack(blocks), jnp.array(wanted)[lax.axis_index("row")], 0, keepdims=False))
    return held


def spread_step(held, one_way=False):
    rows, cols = lax.axis_size("row"), lax.axis_size("col")
    bit = len(held) // 2
    if one_way:
        pairs = [(r * cols + c, r * cols + (c ^ bit)) for r in range(rows) for c in range(cols)
                 if (c ^ source_col(r)) % (2 * bit) == 0]
        moved = lax.ppermute(jnp.stack(held[bit:]), ("row", "col"), pairs)
    else:
        moved = swap(jnp.stack(held[bit:]), "col", bit)
    offset = lax.axis_index("col") ^ source_col(lax.axis_index("row"))
    return [jnp.where(offset & bit != 0, moved[j], held[j]) for j in range(bit)]


def local(inverse_tile, panels, link_panel, diag_inverse, ancestor_tiles):
    rows_axis, cols_axis = lax.axis_size("row"), lax.axis_size("col")
    row_id, col_id = lax.axis_index("row"), lax.axis_index("col")
    siblings, _, local_rows, width = panels.shape
    height, span = diag_inverse.shape[2:]
    row_start = (col_id * rows_axis + row_id) * local_rows
    tile_mask = jnp.repeat(ancestor_tiles, TILE, axis=2)
    kept_rows = lax.dynamic_slice_in_dim(tile_mask, row_start, local_rows, 2).astype(jnp.float32)
    tile = split(inverse_tile).reshape(PARTS, cols_axis, -1, inverse_tile.shape[1])

    def one_pair(panels, kept_first, kept_second, link, given_first, given_second):
        live = {"tile": tile, "given": given_first}
        slots = {}

        def at(slot, *steps):
            slots.setdefault(slot, []).extend(steps)

        late = 2 * span
        pieces = [("first", i, i + late) for i in range(0, width, late)]
        count_first = len(pieces)
        pieces += [("second", i, i + late) for i in range(0, width, late)]
        stages = rows_axis.bit_length() - 1
        second = panels[1] * kept_second - dot(panels[0] * kept_first, link, precise)
        for k, (panel, start, stop) in enumerate(pieces):
            live["piece", k] = panels[0][:, start:stop] * kept_first if panel == "first" else second[:, start:stop]

        def fetch(k, stage):
            if stage == 0:
                live[k, 0] = live.pop(("piece", k))
            for j in reversed(range(1, rows_axis)):
                if j.bit_count() == stage + 1:
                    live[k, j] = swap(live[k, j & (j - 1)], "row", j & -j)

        def blocks(k):
            return [live[k, j] for j in range(rows_axis)]

        def multiply(k):
            gathered = blocks(k)
            if ("sums", k - 1) in live:
                live["sums", k - 1], gathered = lax.optimization_barrier((live["sums", k - 1], gathered))
            live["send", k], live["keep", k] = product(live["tile"], gathered)

        def add_core(k):
            live["sums", k] = live.pop(("keep", k)) + swap(live.pop(("send", k)), "col", 1)

        def add_rest(k):
            live["out", k] = -sum_scatter(live.pop(("sums", k)), "col", 2)

        def collect(k):
            live["own", k] = spread_step(blocks_to_send(blocks(k)), one_way=k >= count_first)

        def spread(k):
            live["own", k] = spread_step(live["own", k])

        def owns(start, stop):
            return jnp.concatenate([live["own", k][0] for k in range(start, stop)], axis=1)

        def outs(start, stop):
            return jnp.concatenate([live["out", k] for k in range(start, stop)], axis=1)

        for k in range(len(pieces)):
            for stage in range(stages):
                at(k + stage, lambda k=k, stage=stage: fetch(k, stage))

        def link_terms():
            link_rows = lax.dynamic_slice_in_dim(link, row_id * height, height, 0)
            link_cols = lax.dynamic_slice_in_dim(link, col_id * span, span, 0)
            given = dot(live["given"], link_cols, precise)
            live["link_cross"] = lax.dynamic_update_slice_in_dim(jnp.zeros_like(link), given, row_id * height, 0)
            live["link_second"] = -dot_tn(link_rows, given, precise)
            for name in ("link_cross", "link_second"):
                live[name] = [by_parity(live[name], odd) for odd in (0, 1)]

        def core_sum(terms):
            sent = swap(terms(1), "col", 1)
            return terms(0) + sent

        def by_rows(sums):
            return sums.reshape(-1, rows_axis, height, sums.shape[1]).swapaxes(0, 1)

        def rest_of_cols(sums):
            return sum_scatter(sums.reshape(-1, cols_axis // 2, span).swapaxes(0, 1), "col", 2)

        def by_parity(array, odd):
            return jnp.concatenate(columns_by_xor(array, odd), axis=1)

        def first_terms():
            out_first = outs(0, count_first)
            own_first, own_second = owns(0, count_first), owns(count_first, len(pieces))
            live["own_second"] = [by_parity(own_second, odd) for odd in (0, 1)]

            def terms(odd):
                cross = dot_tn(out_first, live["own_second"][odd], three_pass) + live["link_cross"][odd]
                return jnp.concatenate([dot_tn(out_first, by_parity(own_first, odd), three_pass), cross])

            live["first_sums"] = sum_step(by_rows(core_sum(terms)), "row", 1)

        def first_sums():
            sums = sum_rows(live["first_sums"], "row", 2)
            live["first_sums"] = rest_of_cols(sums.reshape(-1, sums.shape[2])).reshape(-1, height, span)

        def second_terms():
            out_second = outs(count_first, len(pieces))

            def terms(odd):
                return dot_tn(out_second, live["own_second"][odd], three_pass) + live["link_second"][odd]

            live["second_sum"] = sum_rows(by_rows(rest_of_cols(core_sum(terms))), "row")[0]

        at(1, link_terms)
        last = len(pieces) - 1 + stages
        for k in range(len(pieces)):
            at(k + stages, lambda k=k: collect(k))
            for step in range(1, cols_axis.bit_length() - 1):
                at(k + stages + step, lambda k=k: spread(k))
        for k in range(len(pieces)):
            at(k + stages + 1, lambda k=k: add_core(k))
            at(k + stages, lambda k=k: multiply(k))
        for k in range(len(pieces)):
            at(k + stages + 1, lambda k=k: add_rest(k))
        end = last + 2
        at(last + 1, first_terms)
        at(end, first_sums, second_terms)

        for slot in range(end + 1):
            if slot > 0:
                live = dict(zip(live, lax.optimization_barrier(list(live.values()))))
            for step in slots[slot]:
                step()

        first_sum, cross_sum = live["first_sums"]
        ancestor = jnp.stack([outs(0, count_first), outs(count_first, len(pieces))])
        diagonal = jnp.stack([given_first - first_sum, given_second - live["second_sum"]])
        return ancestor, diagonal, -cross_sum

    results = [one_pair(panels[s], kept_rows[s, 0, :, None], kept_rows[s, 1, :, None], link_panel[s],
                        diag_inverse[s, 0], diag_inverse[s, 1])
               for s in range(siblings)]
    return tuple(jnp.stack(group) for group in zip(*results))


def solution(mesh):
    in_specs = (
        P(("hyp", "row"), "col"),
        P("hyp", None, ("col", "row"), None),
        P("hyp", None, None),
        P("hyp", None, "row", "col"),
        P(),
    )
    out_specs = (
        P("hyp", None, ("row", "col"), None),
        P("hyp", None, "row", "col"),
        P("hyp", "row", "col"),
    )
    return jax.shard_map(local, mesh=mesh, in_specs=in_specs, out_specs=out_specs, check_vma=False)
```
